128 devices in a mesh: comp: 4 (over z_hi, core), tile: 32 (over x, y, z_lo).
Axes of the slice: x: 4, y: 4, z: 4 (z_hi: 2, z_lo: 2; z = z_hi * 2 + z_lo), core: 2. Of those that a mesh axis runs over, the one named last changes fastest.
Arguments:
- state: float32 [4, 4, 31, 12288], P('comp', None, None, 'tile'), may hold values from -6 to 6
- velocity: float32 [4, 2, 31, 12288], P('comp', None, None, 'tile'), may hold values from -4 to 4
- wet_mask: int32 [31, 12288], P(None, 'tile'), may hold values 0 or 1
- margin_source: int32 [4, 32, 279], P('comp', 'tile'), may hold values from 0 to 92
- margin_dest: int32 [4, 32, 279], P('comp', 'tile'), may hold values from 0 to 127, as said below
- margin_block: int32 [4, 32, 279], P('comp', 'tile'), may hold values from 0 to 92
- margin_weight: bfloat16 [4, 32, 279, 128, 128], P('comp', 'tile'), may hold values from -0.375 to 0.375
Outputs:
- new_state: float32 [4, 4, 31, 12288], P('comp', None, None, 'tile')
- coupled_fields: float32 [4, 2, 31, 12288], P('comp', None, None, 'tile')
The draws below stay inside these ranges and needn't reach their ends.
Inputs may be any that keep to these rules, and one draw needn't show every extreme that they name: `margin_dest`: the device numbered c * 32 + t. Rows held by atmosphere devices name ocean devices; rows held by ocean devices name atmosphere devices. A row held by a device of tile index t names a tile index within two of t, counted periodically over the 32 indices. Of one device's 279 rows at most 111 name devices of one tile index, and on every device some tile index is named exactly 111 times.
All inputs are finite; a program needn't handle non-finite values. No bound on the sum of `wet_mask` on one device may be relied on, other than what follows from the above.
Results may differ from the reference program's by a relative error of at most 0.0029.
Values sent between devices are 32-bit elements; how exact they have to be, the bound alone decides.
A program may use at most 64 MiB of HBM per device.

```python
import jax
import jax.numpy as jnp
import numpy as np
from jax import lax

KB = 128
NY = 31
NX = 384
NB = 93
OV = 279
CAP = 111
N_COMP = 4
N_TILE = 32


def draw_margin_dest(key, part):
    key = jax.random.fold_in(key, 17)
    keys = jax.random.split(key, 5)
    slots = 5 * CAP
    base = jnp.array([1, 2, 3, 2, 1], jnp.int32)
    levels = base[None, None, :] + jax.random.randint(keys[0], (N_COMP, N_TILE, 5), 0, 2)
    chosen = jax.random.randint(keys[1], (N_COMP, N_TILE, 1), 0, 5)
    levels = jnp.where(jnp.arange(5)[None, None, :] == chosen, 8, levels)
    slot_index = jnp.arange(slots)
    slot_rel = slot_index // CAP
    noise = jax.random.randint(keys[2], (N_COMP, N_TILE, slots), 0, 1024)
    score = levels[:, :, slot_rel] * 4194304 + noise * 4096 + slot_index
    picked = lax.top_k(score, OV)[1]
    rel_of = picked // CAP
    shuffle = jax.random.randint(keys[3], (N_COMP, N_TILE, OV), 0, 1048576) * 1024 + jnp.arange(OV)
    order = jnp.argsort(shuffle, axis=-1)
    rel_of = jnp.take_along_axis(rel_of, order, -1)
    own_tile = jnp.arange(N_TILE)[None, :, None]
    tile_of = (own_tile + rel_of - 2 + N_TILE) % N_TILE
    ocean_comp = jax.random.randint(keys[4], (N_COMP, N_TILE, OV), 0, N_COMP - 1)
    sender = jnp.arange(N_COMP)[:, None, None]
    comp_of = jnp.where(sender == N_COMP - 1, ocean_comp, N_COMP - 1)
    return (comp_of * N_TILE + tile_of).astype(jnp.int32)


def place_ends(values, key, least, top_value):
    longest = values.shape.index(max(values.shape))
    spots = []
    for shift in (0, 1):
        where = [jax.random.randint(jax.random.fold_in(key, axis), (), 0, length) for axis, length in enumerate(values.shape)]
        where[longest] = (where[longest] + shift) % values.shape[longest]
        spots.append(tuple(where))
    return values.at[spots[0]].set(least).at[spots[1]].set(top_value)


def shard_levels(rng, dims, shards, least, largest):
    def one(dim, blocks):
        heights = jax.random.uniform(jax.random.fold_in(jax.random.fold_in(rng, 6), dim), (blocks,), jnp.float32, least / len(shards), largest / len(shards))
        return jnp.repeat(jnp.exp(heights), dims[dim] // blocks).reshape((-1,) + (1,) * (len(dims) - dim - 1))

    level = one(*shards[0])
    for cut in shards[1:]:
        level = level * one(*cut)
    return level


def centred(key, shape, scale, reach, cuts=(), held_as=jnp.bfloat16):
    entries = scale * jax.random.normal(key, shape, jnp.float32)
    if cuts:
        entries = entries * shard_levels(key, shape, cuts, -0.22, 0.18)
    return jnp.clip(entries, -reach, reach).astype(held_as)


def setup_inputs(seed: int = 0) -> dict:
    splits = jax.random.split(jax.random.key(seed), 8)
    state = centred(splits[0], (N_COMP, 4, NY, N_TILE * NX), 1.0, 6.0, ((0, 4), (3, 32)), jnp.float32)
    velocity = centred(splits[1], (N_COMP, 2, NY, N_TILE * NX), 1.0, 4.0, ((0, 4), (3, 32)), jnp.float32)
    wet_mask = place_ends((jax.random.randint(splits[2], (NY, N_TILE * NX), 0, 4) < 3).astype(jnp.int32), jax.random.fold_in(splits[2], 1), 0, 1)
    margin_source = place_ends(jax.random.randint(splits[3], (N_COMP, N_TILE, OV), 0, NB), jax.random.fold_in(splits[3], 1), 0, NB - 1).astype(jnp.int32)
    margin_dest = draw_margin_dest(jax.random.fold_in(splits[7], 71), 0)
    margin_block = place_ends(jax.random.randint(splits[5], (N_COMP, N_TILE, OV), 0, NB), jax.random.fold_in(splits[5], 1), 0, NB - 1).astype(jnp.int32)
    margin_weight = centred(splits[6], (N_COMP, N_TILE, OV, KB, KB), (2 * KB) ** -0.5, 0.375, ((0, 4), (1, 32)))
    return {"state": state, "velocity": velocity, "wet_mask": wet_mask, "margin_source": margin_source, "margin_dest": margin_dest, "margin_block": margin_block, "margin_weight": margin_weight}


atmos_step = 0.02
viscosity = 0.3
ocean_step = 0.1
diffusivity = 0.2
vertical_mix = 0.5
heat_coef = 0.5
salt_coef = 0.5

def gll_tables():
    nodes = np.array([-1.0, -1.0 / np.sqrt(5.0), 1.0 / np.sqrt(5.0), 1.0])
    weights = np.array([1.0 / 6.0, 5.0 / 6.0, 5.0 / 6.0, 1.0 / 6.0])
    legendre = (5.0 * nodes ** 3 - 3.0 * nodes) / 2.0
    deriv = np.zeros((4, 4))
    for row_node in range(4):
        for col_node in range(4):
            if row_node != col_node:
                deriv[row_node, col_node] = legendre[row_node] / (legendre[col_node] * (nodes[row_node] - nodes[col_node]))
    deriv[0, 0] = -3.0
    deriv[3, 3] = 3.0
    return (jnp.asarray(deriv, jnp.float32), jnp.asarray(weights, jnp.float32))

def element_view(grid, start, count, rows):
    elem_rows = (rows - 1) // 3
    return jnp.stack([jnp.stack([grid[..., i:i + 3 * elem_rows - 2:3, start + j:start + j + 3 * count - 2:3] for j in range(4)], -3) for i in range(4)], -4)

def assemble(parts, rows, start, count):
    elem_rows = (rows - 1) // 3
    total = jnp.zeros(parts.shape[:-4] + (rows, start + 3 * count + 1), jnp.float32)
    for i in range(4):
        for j in range(4):
            total = total.at[..., i:i + 3 * elem_rows - 2:3, start + j:start + j + 3 * count - 2:3].add(parts[..., i, j, :, :])
    return total

def element_tendency(values, winds, deriv, weights):
    high = lax.Precision.HIGHEST
    along_x = jnp.einsum('jm,limye->lijye', deriv, values, precision=high)
    along_y = jnp.einsum('im,lmjye->lijye', deriv, values, precision=high)
    mass_local = (weights[:, None] * weights[None, :] / 4.0)[:, :, None, None]
    advect = 2.0 * (winds[0] * along_x + winds[1] * along_y)
    weighted = weights[:, None] * deriv
    stiff_x = weights[:, None, None, None] * jnp.einsum('kj,likye->lijye', weighted, along_x, precision=high)
    stiff_y = weights[None, :, None, None] * jnp.einsum('ki,lkjye->lijye', weighted, along_y, precision=high)
    return -mass_local * advect - viscosity * (stiff_x + stiff_y)

def atmos_band(prognostic, winds):
    rows = prognostic.shape[1]
    width = prognostic.shape[2]
    count = width // 3
    deriv, weights = gll_tables()
    ext_values = jnp.concatenate([prognostic, prognostic[..., :1]], -1)
    ext_winds = jnp.concatenate([winds, winds[..., :1]], -1)
    tend = element_tendency(element_view(ext_values, 0, count, rows), element_view(ext_winds, 0, count, rows), deriv, weights)
    total = assemble(tend, rows, 0, count)
    total = total[..., :width].at[..., 0].add(total[..., width])
    mass_local = (weights[:, None] * weights[None, :] / 4.0)[:, :, None, None] * jnp.ones(((rows - 1) // 3, count), jnp.float32)
    mass = assemble(mass_local, rows, 0, count)
    mass = mass[..., :width].at[..., 0].add(mass[..., width])
    return prognostic + atmos_step * total / mass

def ocean_global(tracer, winds, wet, forcing):
    east_u = winds[0]
    north_v = winds[1]
    right = jnp.roll(tracer, -1, -1)
    right_u = jnp.roll(east_u, -1, -1)
    right_wet = jnp.roll(wet, -1, -1)
    flux_x = wet * right_wet * (0.25 * (east_u + right_u) * (tracer + right) - diffusivity * (right - tracer))
    div_x = flux_x - jnp.roll(flux_x, 1, -1)
    flux_y = wet[:-1] * wet[1:] * (0.25 * (north_v[:-1] + north_v[1:]) * (tracer[:, :-1] + tracer[:, 1:]) - diffusivity * (tracer[:, 1:] - tracer[:, :-1]))
    padded = jnp.pad(flux_y, ((0, 0), (1, 1), (0, 0)))
    div_y = padded[:, 1:] - padded[:, :-1]
    vertical = vertical_mix * (tracer[jnp.array([1, 0, 3, 2])] - tracer)
    return tracer + wet * ocean_step * (-div_x - div_y + vertical + forcing)

def reference(state, velocity, wet_mask, margin_source, margin_dest, margin_block, margin_weight):
    devices = N_COMP * N_TILE
    local = state.reshape(N_COMP, 4, NY, N_TILE, NX).transpose(0, 3, 1, 2, 4)
    surface = jnp.stack([local[:, :, 0], local[:, :, 2]], 2)
    payload = surface.reshape(devices, 2, NB, KB).astype(jnp.bfloat16)

    def one_device(args):
        blocks, sources, weights = args
        picked = blocks[:, sources].astype(jnp.float32)
        return jnp.einsum('aok,okj->oaj', picked, weights.astype(jnp.float32), precision=lax.Precision.HIGHEST)
    pieces = lax.map(one_device, (payload, margin_source.reshape(devices, OV), margin_weight.reshape(devices, OV, KB, KB)))
    codes = (margin_dest * NB + margin_block).reshape(-1).astype(jnp.int32)
    summed = jax.ops.segment_sum(pieces.reshape(-1, 2 * KB), codes, num_segments=devices * NB)
    coupled = summed.reshape(N_COMP, N_TILE, NB, 2, KB).transpose(0, 1, 3, 2, 4).reshape(N_COMP, N_TILE, 2, NY, NX)
    coupled = coupled.transpose(0, 2, 3, 1, 4).reshape(N_COMP, 2, NY, N_TILE * NX)
    bands = [atmos_band(state[band], velocity[band]) for band in range(N_COMP - 1)]
    tracer = state[N_COMP - 1]
    zeros = jnp.zeros_like(tracer[0])
    forcing = jnp.stack([heat_coef * (coupled[N_COMP - 1, 0] - tracer[0]), zeros, salt_coef * (coupled[N_COMP - 1, 1] - tracer[2]), zeros])
    ocean = ocean_global(tracer, velocity[N_COMP - 1], wet_mask.astype(jnp.float32), forcing)
    new_state = jnp.stack(bands + [ocean])
    return (new_state, coupled)
```

```python
import functools

import jax
import jax.numpy as jnp
import numpy as np
from jax import lax
from jax.experimental import pallas as pl
from jax.experimental.pallas import tpu as pltpu
from jax.sharding import PartitionSpec as P

MESH = pl.DeviceIdType.MESH

atmos_step = 0.02
viscosity = 0.3
ocean_step = 0.1
diffusivity = 0.2
vertical_mix = 0.5
heat_coef = 0.5
salt_coef = 0.5

LANES = 128
GROUP = 8
CHUNK = 40
OFFSETS = (0, 4, 1, 3, 2)


def gll_tables():
    nodes = np.array([-1.0, -1.0 / np.sqrt(5.0), 1.0 / np.sqrt(5.0), 1.0])
    weights = np.array([1.0 / 6.0, 5.0 / 6.0, 5.0 / 6.0, 1.0 / 6.0])
    legendre = (5.0 * nodes**3 - 3.0 * nodes) / 2.0
    deriv = np.zeros((4, 4))
    for row_node in range(4):
        for col_node in range(4):
            if row_node != col_node:
                deriv[row_node, col_node] = legendre[row_node] / (
                    legendre[col_node] * (nodes[row_node] - nodes[col_node])
                )
    deriv[0, 0] = -3.0
    deriv[3, 3] = 3.0
    return deriv, weights


def stencils():
    deriv, weights = gll_tables()
    stiff = np.einsum("k,kj,km->jm", weights, deriv, deriv)
    derivative = np.zeros((5, 7))
    stiffness = np.zeros((5, 7))
    for kind, holders in enumerate(((0, 3), (1,), (2,), (0,), (3,))):
        total = sum(weights[j] for j in holders)
        for j in holders:
            for m in range(4):
                derivative[kind, m - j + 3] += weights[j] * deriv[j, m] / total
                stiffness[kind, m - j + 3] += stiff[j, m] / total
    return derivative, stiffness


def by_kind(kinds, values):
    out = jnp.full(kinds.shape, float(values[0]), jnp.float32)
    for kind in range(1, len(values)):
        out = jnp.where(kinds == kind, float(values[kind]), out)
    return out


def kernel(
    sizes,
    state_hbm,
    velocity_hbm,
    wet_hbm,
    source_hbm,
    dest_hbm,
    block_hbm,
    weight_hbm,
    new_ref,
    coupled_ref,
    state,
    velocity,
    wet,
    source,
    dest,
    block,
    weight,
    payload,
    picked,
    pieces,
    fields,
    strips,
    edges,
    outbox,
    inbox,
    load_sem,
    chunk_sem,
    out_sem,
    in_sem,
    strip_sem,
    edge_sem,
):
    comps, tiles, rows, width, margins = sizes
    ocean = comps - 1
    padded = rows + 1
    parts = width // LANES
    span = parts * padded
    wide = width + LANES
    me = lax.axis_index("comp")
    tile = lax.axis_index("tile")

    def tile_at(step):
        return lax.rem(tile + step + tiles, tiles)

    def device(comp, step):
        return {"comp": comp, "tile": tile_at(step)}

    barrier = pltpu.get_barrier_semaphore()

    def greet(comp, step):
        pl.semaphore_signal(
            barrier, inc=1, device_id=device(comp, step), device_id_type=MESH
        )

    greet(me, -1)
    greet(me, 1)

    @pl.when(me == ocean)
    def _():
        for k in range(5):
            for comp in range(ocean):
                greet(comp, k - 2)

    @pl.when(me != ocean)
    def _():
        for k in range(5):
            greet(ocean, k - 2)

    loads = [
        pltpu.make_async_copy(src, dst, load_sem.at[i])
        for i, (src, dst) in enumerate(
            (
                (source_hbm, source),
                (state_hbm, state),
                (dest_hbm, dest),
                (block_hbm, block),
                (velocity_hbm, velocity),
                (wet_hbm, wet),
            )
        )
    ]
    bounds = [(low, min(low + CHUNK, margins)) for low in range(0, margins, CHUNK)]
    chunks = [
        pltpu.make_async_copy(
            weight_hbm.at[0, 0, pl.ds(low, high - low)],
            weight.at[pl.ds(low, high - low)],
            chunk_sem.at[i],
        )
        for i, (low, high) in enumerate(bounds)
    ]
    for copy in loads[:4] + chunks + loads[4:]:
        copy.start()

    payload[...] = jnp.zeros_like(payload)
    pieces[pl.ds(margins // 8 * 8, pieces.shape[0] - margins // 8 * 8), :] = jnp.zeros(
        (pieces.shape[0] - margins // 8 * 8, 2 * LANES), jnp.float32
    )
    loads[0].wait()
    loads[1].wait()
    for a in range(2):
        for part in range(parts):
            payload[pl.ds(part * padded, rows), pl.ds(a * LANES, LANES)] = state[
                0, 2 * a, :, pl.ds(part * LANES, LANES)
            ]

    def place_of(numbers):
        row = (numbers * 171) >> 9
        return (numbers - 3 * row) * padded + row

    slots = lax.broadcasted_iota(jnp.int32, (span, margins), 0)
    chosen = (slots == place_of(source[0])).astype(jnp.float32)
    picked[pl.ds(0, margins), :] = lax.dot_general(
        chosen.T.astype(jnp.bfloat16),
        payload[...].astype(jnp.bfloat16),
        (((1,), (0,)), ((), ())),
        preferred_element_type=jnp.float32,
    )

    for s in range(4):
        fields[s, pl.ds(0, rows), pl.ds(0, width)] = state[0, s]
    loads[4].wait()
    loads[5].wait()
    fields[4, pl.ds(0, rows), pl.ds(0, width)] = velocity[0, 0]
    fields[5, pl.ds(0, rows), pl.ds(0, width)] = wet[...].astype(jnp.float32)
    fields[6, pl.ds(0, rows), pl.ds(0, width)] = velocity[0, 1]
    for s in range(7):
        fields[s, pl.ds(rows, 1), pl.ds(0, width)] = jnp.zeros((1, width), jnp.float32)
    lane = lax.broadcasted_iota(jnp.int32, (padded, LANES), 1)
    right_going = fields[0, :, pl.ds(width - LANES, LANES)]
    left_going = fields[0, :, pl.ds(0, LANES)]
    for s in range(1, 6):
        moved = pltpu.roll(fields[s, :, pl.ds(width - LANES, LANES)], LANES - 4 * s, 1)
        right_going = jnp.where(lane < LANES - 4 * s, moved, right_going)
        moved = pltpu.roll(fields[s, :, pl.ds(0, LANES)], 4 * s, 1)
        left_going = jnp.where(lane >= 4 * s, moved, left_going)
    strips[0] = right_going
    strips[1] = left_going

    rank = lax.rem(lax.broadcasted_iota(jnp.int32, (2 * GROUP, LANES), 0), GROUP)
    for (low, high), copy in zip(bounds, chunks):
        copy.wait()
        for first in range(low, high, GROUP):
            count = min(GROUP, high - first)
            held = jnp.concatenate(
                [picked[pl.ds(first, GROUP), pl.ds(a * LANES, LANES)] for a in range(2)], 0
            )
            spread = jnp.concatenate(
                [jnp.where(rank == i, held, 0.0).astype(jnp.bfloat16) for i in range(count)], 1
            )
            product = jnp.dot(
                spread,
                weight[pl.ds(first, count)].reshape(count * LANES, LANES),
                preferred_element_type=jnp.float32,
            )
            for a in range(2):
                pieces[pl.ds(first, count), pl.ds(a * LANES, LANES)] = product[
                    a * GROUP : a * GROUP + count
                ]

    loads[2].wait()
    loads[3].wait()
    target = dest[0]
    offset = (target & (tiles - 1)) - tile + 2
    offset = jnp.where(offset < 0, offset + tiles, offset)
    offset = jnp.where(offset >= tiles, offset - tiles, offset)
    place = place_of(block[0])
    whole = pieces[...]
    coarse = whole.astype(jnp.bfloat16)
    fine = (whole - coarse.astype(jnp.float32)).astype(jnp.bfloat16)

    def gathered(codes, low, count):
        numbers = lax.broadcasted_iota(jnp.int32, (count, margins), 0) + low
        onehot = (numbers == codes).astype(jnp.float32).astype(jnp.bfloat16)
        return jnp.dot(
            onehot, coarse[:margins], preferred_element_type=jnp.float32
        ) + jnp.dot(onehot, fine[:margins], preferred_element_type=jnp.float32)

    def message(slot, far_slot, comp, k):
        return pltpu.make_async_remote_copy(
            src_ref=outbox.at[slot],
            dst_ref=inbox.at[far_slot],
            send_sem=out_sem.at[slot],
            recv_sem=in_sem.at[far_slot],
            device_id=device(comp, k - 2),
            device_id_type=MESH,
        )

    def strip(side):
        return pltpu.make_async_remote_copy(
            src_ref=strips.at[side],
            dst_ref=edges.at[side],
            send_sem=strip_sem.at[side],
            recv_sem=edge_sem.at[side],
            device_id=device(me, 1 - 2 * side),
            device_id_type=MESH,
        )

    @pl.when(me == ocean)
    def _():
        pl.semaphore_wait(barrier, 2 + 5 * ocean)
        codes = (offset * ocean + (target >> 5)) * span + place
        for k in OFFSETS:
            out = gathered(codes, k * ocean * span, ocean * span)
            for comp in range(ocean):
                outbox[comp * 5 + k] = out[comp * span : (comp + 1) * span]
                message(comp * 5 + k, k, comp, k).start()

    @pl.when(me != ocean)
    def _():
        pl.semaphore_wait(barrier, 2 + 5)
        codes = offset * span + place
        for k in OFFSETS:
            outbox[k] = gathered(codes, k * span, span)
            message(k, me * 5 + k, ocean, k).start()

    for side in range(2):
        strip(side).start()
    for side in range(2):
        strip(side).wait()

    for s in range(6):
        after = pltpu.roll(edges[1], (LANES - 4 * s) % LANES, 1)
        before = pltpu.roll(edges[0], 4 * s, 1)
        fields[s, :, pl.ds(width, LANES)] = jnp.where(
            lane == 0, after, jnp.where(lane >= LANES - 3, before, 0.0)
        )

    def total(count):
        out = None
        for slot in range(count):
            pltpu.make_async_copy(inbox.at[slot], inbox.at[slot], in_sem.at[slot]).wait()
            out = inbox[slot] if out is None else out + inbox[slot]
        return out

    def give(out):
        for a in range(2):
            for part in range(parts):
                coupled_ref[0, a, :, pl.ds(part * LANES, LANES)] = out[
                    part * padded : part * padded + rows, a * LANES : (a + 1) * LANES
                ]

    def sent(count):
        for slot in range(count):
            pltpu.make_async_copy(
                outbox.at[slot], outbox.at[slot], out_sem.at[slot]
            ).wait()

    @pl.when(me != ocean)
    def _():
        derivative, stiffness = stencils()
        columns = lax.rem(lax.broadcasted_iota(jnp.int32, (padded, width), 1), 3)
        row = lax.broadcasted_iota(jnp.int32, (padded, width), 0)
        row_kind = lax.rem(row, 3)
        row_kind = jnp.where(row == 0, 3, jnp.where(row == rows - 1, 4, row_kind))
        east = fields[4, :, pl.ds(0, width)]
        north = fields[6, :, pl.ds(0, width)]
        for s in range(4):
            along_x = along_y = stiff = None
            whole = fields[s]
            centre = fields[s, :, pl.ds(0, width)]
            for k in range(7):
                step = k - 3
                shifted = whole if step == 0 else pltpu.roll(whole, (-step) % wide, 1)
                shifted = shifted[:, :width]
                first = by_kind(columns, derivative[:3, k]) * shifted
                second = by_kind(columns, stiffness[:3, k]) * shifted
                shifted = centre if step == 0 else pltpu.roll(centre, (-step) % padded, 0)
                third = by_kind(row_kind, derivative[:, k]) * shifted
                second += by_kind(row_kind, stiffness[:, k]) * shifted
                along_x = first if k == 0 else along_x + first
                along_y = third if k == 0 else along_y + third
                stiff = second if k == 0 else stiff + second
            out = centre - atmos_step * (
                2.0 * (east * along_x + north * along_y) + 4.0 * viscosity * stiff
            )
            new_ref[0, s] = out[:rows]
        give(total(5))
        sent(5)

    @pl.when(me == ocean)
    def _():
        p = fields[4]
        m = fields[5]
        m_centre = m[:, :width]
        q = fields[6, :, pl.ds(0, width)]
        m_x = m * pltpu.roll(m, wide - 1, 1)
        p_x = 0.25 * (p + pltpu.roll(p, wide - 1, 1))
        m_y = m_centre * pltpu.roll(m_centre, padded - 1, 0)
        q_y = 0.25 * (q + pltpu.roll(q, padded - 1, 0))
        base = []
        for s in range(4):
            u = fields[s]
            u_next = pltpu.roll(u, wide - 1, 1)
            flux = m_x * (p_x * (u + u_next) - diffusivity * (u_next - u))
            change = (flux - pltpu.roll(flux, 1, 1))[:, :width]
            u = u[:, :width]
            u_next = pltpu.roll(u, padded - 1, 0)
            flux = m_y * (q_y * (u + u_next) - diffusivity * (u_next - u))
            change = change + (flux - pltpu.roll(flux, 1, 0))
            other = fields[s ^ 1, :, pl.ds(0, width)]
            step = vertical_mix * (other - u) - change
            fields[s, :, pl.ds(0, width)] = u
            base.append(step)
        for s in (1, 3):
            u = fields[s, :, pl.ds(0, width)]
            new_ref[0, s] = (u + m_centre * (ocean_step * base[s]))[:rows]
        out = total(5 * ocean)
        give(out)
        for a, coef in ((0, heat_coef), (1, salt_coef)):
            s = 2 * a
            u = fields[s, :, pl.ds(0, width)]
            surface = jnp.concatenate(
                [
                    out[part * padded : (part + 1) * padded, a * LANES : (a + 1) * LANES]
                    for part in range(parts)
                ],
                1,
            )
            step = base[s] + coef * (surface - u)
            new_ref[0, s] = (u + m_centre * (ocean_step * step))[:rows]
        sent(5 * ocean)


def local(sizes, *arrays):
    comps, tiles, rows, width, margins = sizes
    parts = width // LANES
    padded = rows + 1
    span = parts * padded
    chunks = -(-margins // CHUNK)
    roomy = -(-margins // LANES) * LANES
    state, velocity, wet = arrays[:3]
    slots = 5 * (comps - 1)
    return pl.pallas_call(
        functools.partial(kernel, sizes),
        out_shape=(
            jax.ShapeDtypeStruct(state.shape, jnp.float32),
            jax.ShapeDtypeStruct(velocity.shape, jnp.float32),
        ),
        in_specs=[pl.BlockSpec(memory_space=pl.ANY)] * len(arrays),
        out_specs=(pl.BlockSpec(memory_space=pltpu.VMEM),) * 2,
        scratch_shapes=[
            *[pltpu.VMEM(array.shape, array.dtype) for array in arrays[:6]],
            pltpu.VMEM(arrays[6].shape[2:], jnp.bfloat16),
            pltpu.VMEM((span, 2 * LANES), jnp.float32),
            pltpu.VMEM((roomy, 2 * LANES), jnp.float32),
            pltpu.VMEM((roomy, 2 * LANES), jnp.float32),
            pltpu.VMEM((7, padded, width + LANES), jnp.float32),
            pltpu.VMEM((2, padded, LANES), jnp.float32),
            pltpu.VMEM((2, padded, LANES), jnp.float32),
            pltpu.VMEM((slots, span, 2 * LANES), jnp.float32),
            pltpu.VMEM((slots, span, 2 * LANES), jnp.float32),
            pltpu.SemaphoreType.DMA((6,)),
            pltpu.SemaphoreType.DMA((chunks,)),
            pltpu.SemaphoreType.DMA((slots,)),
            pltpu.SemaphoreType.DMA((slots,)),
            pltpu.SemaphoreType.DMA((2,)),
            pltpu.SemaphoreType.DMA((2,)),
        ],
        compiler_params=pltpu.CompilerParams(
            collective_id=0, has_side_effects=True, vmem_limit_bytes=56 * 2**20
        ),
    )(*arrays)


def solution(mesh):
    comps, tiles = mesh.shape["comp"], mesh.shape["tile"]

    def whole(*arrays):
        rows, width = arrays[0].shape[2:]
        sizes = (comps, tiles, rows, width // tiles, arrays[3].shape[-1])
        placed = (
            P("comp", None, None, "tile"),
            P("comp", None, None, "tile"),
            P(None, "tile"),
            P("comp", "tile", None),
            P("comp", "tile", None),
            P("comp", "tile", None),
            P("comp", "tile", None, None, None),
        )
        return jax.shard_map(
            functools.partial(local, sizes),
            mesh=mesh,
            in_specs=placed,
            out_specs=(P("comp", None, None, "tile"), P("comp", None, None, "tile")),
            check_vma=False,
        )(*arrays)

    return whole
```

```python
import functools

import jax
import jax.numpy as jnp
import numpy as np
from jax import lax
from jax.experimental import pallas as pl
from jax.experimental.pallas import tpu as pltpu
from jax.sharding import PartitionSpec as P

MESH = pl.DeviceIdType.MESH

atmos_step = 0.02
viscosity = 0.3
ocean_step = 0.1
diffusivity = 0.2
vertical_mix = 0.5
heat_coef = 0.5
salt_coef = 0.5

LANES = 128
GROUP = 8
CHUNK = 40
OFFSETS = (0, 4, 1, 3, 2)


def gll_tables():
    nodes = np.array([-1.0, -1.0 / np.sqrt(5.0), 1.0 / np.sqrt(5.0), 1.0])
    weights = np.array([1.0 / 6.0, 5.0 / 6.0, 5.0 / 6.0, 1.0 / 6.0])
    legendre = (5.0 * nodes**3 - 3.0 * nodes) / 2.0
    deriv = np.zeros((4, 4))
    for row_node in range(4):
        for col_node in range(4):
            if row_node != col_node:
                deriv[row_node, col_node] = legendre[row_node] / (
                    legendre[col_node] * (nodes[row_node] - nodes[col_node])
                )
    deriv[0, 0] = -3.0
    deriv[3, 3] = 3.0
    return deriv, weights


def stencils():
    deriv, weights = gll_tables()
    stiff = np.einsum("k,kj,km->jm", weights, deriv, deriv)
    derivative = np.zeros((5, 7))
    stiffness = np.zeros((5, 7))
    for kind, holders in enumerate(((0, 3), (1,), (2,), (0,), (3,))):
        total = sum(weights[j] for j in holders)
        for j in holders:
            for m in range(4):
                derivative[kind, m - j + 3] += weights[j] * deriv[j, m] / total
                stiffness[kind, m - j + 3] += stiff[j, m] / total
    return derivative, stiffness


def by_kind(kinds, values):
    out = jnp.full(kinds.shape, float(values[0]), jnp.float32)
    for kind in range(1, len(values)):
        out = jnp.where(kinds == kind, float(values[kind]), out)
    return out


def kernel(
    sizes,
    state_hbm,
    velocity_hbm,
    wet_hbm,
    source_hbm,
    dest_hbm,
    block_hbm,
    weight_hbm,
    new_hbm,
    coupled_hbm,
    state,
    velocity,
    wet,
    source,
    dest,
    block,
    weight,
    payload,
    picked,
    pieces,
    fields,
    strips,
    edges,
    outbox,
    inbox,
    load_sem,
    chunk_sem,
    out_sem,
    in_sem,
    strip_sem,
    edge_sem,
):
    comps, tiles, rows, width, margins = sizes
    ocean = comps - 1
    padded = rows + 1
    parts = width // LANES
    span = parts * padded
    wide = width + LANES
    me = lax.axis_index("comp")
    tile = lax.axis_index("tile")

    def tile_at(step):
        return lax.rem(tile + step + tiles, tiles)

    def device(comp, step):
        return {"comp": comp, "tile": tile_at(step)}

    barrier = pltpu.get_barrier_semaphore()

    def greet(comp, step):
        pl.semaphore_signal(
            barrier, inc=1, device_id=device(comp, step), device_id_type=MESH
        )

    greet(me, -1)
    greet(me, 1)

    @pl.when(me == ocean)
    def _():
        for k in range(5):
            for comp in range(ocean):
                greet(comp, k - 2)

    @pl.when(me != ocean)
    def _():
        for k in range(5):
            greet(ocean, k - 2)

    loads = [
        pltpu.make_async_copy(src, dst, load_sem.at[i])
        for i, (src, dst) in enumerate(
            (
                (source_hbm, source),
                (state_hbm.at[0, :, 0, :], state.at[0]),
                (state_hbm.at[0, :, 2, :], state.at[2]),
                (dest_hbm, dest),
                (block_hbm, block),
                (state_hbm.at[0, :, 1, :], state.at[1]),
                (state_hbm.at[0, :, 3, :], state.at[3]),
                (velocity_hbm.at[0, :, 0, :], velocity.at[0]),
                (velocity_hbm.at[0, :, 1, :], velocity.at[1]),
                (wet_hbm, wet),
            )
        )
    ]
    bounds = [(low, min(low + CHUNK, margins)) for low in range(0, margins, CHUNK)]
    chunks = [
        pltpu.make_async_copy(
            weight_hbm.at[0, 0, pl.ds(low, high - low)],
            weight.at[pl.ds(low, high - low)],
            chunk_sem.at[i],
        )
        for i, (low, high) in enumerate(bounds)
    ]
    for copy in loads[:5] + chunks + loads[5:]:
        copy.start()

    payload[...] = jnp.zeros_like(payload)
    pieces[pl.ds(margins // 8 * 8, pieces.shape[0] - margins // 8 * 8), :] = jnp.zeros(
        (pieces.shape[0] - margins // 8 * 8, 2 * LANES), jnp.float32
    )
    for copy in loads[:3]:
        copy.wait()
    for a in range(2):
        for part in range(parts):
            payload[pl.ds(part * padded, rows), pl.ds(a * LANES, LANES)] = state[
                2 * a, :, pl.ds(part * LANES, LANES)
            ]

    def place_of(numbers):
        row = (numbers * 171) >> 9
        return (numbers - 3 * row) * padded + row

    slots = lax.broadcasted_iota(jnp.int32, (span, margins), 0)
    chosen = (slots == place_of(source[0])).astype(jnp.float32)
    picked[pl.ds(0, margins), :] = lax.dot_general(
        chosen.T.astype(jnp.bfloat16),
        payload[...].astype(jnp.bfloat16),
        (((1,), (0,)), ((), ())),
        preferred_element_type=jnp.float32,
    )

    for copy in loads[5:]:
        copy.wait()
    for s in range(4):
        fields[s, pl.ds(0, rows), pl.ds(0, width)] = state[s]
    fields[4, pl.ds(0, rows), pl.ds(0, width)] = velocity[0]
    fields[5, pl.ds(0, rows), pl.ds(0, width)] = wet[...].astype(jnp.float32)
    fields[6, pl.ds(0, rows), pl.ds(0, width)] = velocity[1]
    for s in range(7):
        fields[s, pl.ds(rows, 1), pl.ds(0, width)] = jnp.zeros((1, width), jnp.float32)
    lane = lax.broadcasted_iota(jnp.int32, (padded, LANES), 1)
    right_going = fields[0, :, pl.ds(width - LANES, LANES)]
    left_going = fields[0, :, pl.ds(0, LANES)]
    for s in range(1, 6):
        moved = pltpu.roll(fields[s, :, pl.ds(width - LANES, LANES)], LANES - 4 * s, 1)
        right_going = jnp.where(lane < LANES - 4 * s, moved, right_going)
        moved = pltpu.roll(fields[s, :, pl.ds(0, LANES)], 4 * s, 1)
        left_going = jnp.where(lane >= 4 * s, moved, left_going)
    strips[0] = right_going
    strips[1] = left_going

    rank = lax.rem(lax.broadcasted_iota(jnp.int32, (2 * GROUP, LANES), 0), GROUP)
    for (low, high), copy in zip(bounds, chunks):
        copy.wait()
        for first in range(low, high, GROUP):
            count = min(GROUP, high - first)
            held = jnp.concatenate(
                [picked[pl.ds(first, GROUP), pl.ds(a * LANES, LANES)] for a in range(2)], 0
            )
            spread = jnp.concatenate(
                [jnp.where(rank == i, held, 0.0).astype(jnp.bfloat16) for i in range(count)], 1
            )
            product = jnp.dot(
                spread,
                weight[pl.ds(first, count)].reshape(count * LANES, LANES),
                preferred_element_type=jnp.float32,
            )
            for a in range(2):
                pieces[pl.ds(first, count), pl.ds(a * LANES, LANES)] = product[
                    a * GROUP : a * GROUP + count
                ]

    loads[3].wait()
    loads[4].wait()
    target = dest[0]
    offset = (target & (tiles - 1)) - tile + 2
    offset = jnp.where(offset < 0, offset + tiles, offset)
    offset = jnp.where(offset >= tiles, offset - tiles, offset)
    place = place_of(block[0])
    whole = pieces[...]
    coarse = whole.astype(jnp.bfloat16)
    fine = (whole - coarse.astype(jnp.float32)).astype(jnp.bfloat16)

    def gathered(codes, low, count):
        numbers = lax.broadcasted_iota(jnp.int32, (count, margins), 0) + low
        onehot = (numbers == codes).astype(jnp.float32).astype(jnp.bfloat16)
        return jnp.dot(
            onehot, coarse[:margins], preferred_element_type=jnp.float32
        ) + jnp.dot(onehot, fine[:margins], preferred_element_type=jnp.float32)

    def message(slot, far_slot, comp, k):
        return pltpu.make_async_remote_copy(
            src_ref=outbox.at[slot],
            dst_ref=inbox.at[far_slot],
            send_sem=out_sem.at[slot],
            recv_sem=in_sem.at[far_slot],
            device_id=device(comp, k - 2),
            device_id_type=MESH,
        )

    def strip(side):
        return pltpu.make_async_remote_copy(
            src_ref=strips.at[side],
            dst_ref=edges.at[side],
            send_sem=strip_sem.at[side],
            recv_sem=edge_sem.at[side],
            device_id=device(me, 1 - 2 * side),
            device_id_type=MESH,
        )

    @pl.when(me == ocean)
    def _():
        pl.semaphore_wait(barrier, 2 + 5 * ocean)
        codes = (offset * ocean + (target >> 5)) * span + place
        for k in OFFSETS:
            out = gathered(codes, k * ocean * span, ocean * span)
            for comp in range(ocean):
                outbox[comp * 5 + k] = out[comp * span : (comp + 1) * span]
                message(comp * 5 + k, k, comp, k).start()

    @pl.when(me != ocean)
    def _():
        pl.semaphore_wait(barrier, 2 + 5)
        codes = offset * span + place
        for k in OFFSETS:
            outbox[k] = gathered(codes, k * span, span)
            message(k, me * 5 + k, ocean, k).start()

    for side in range(2):
        strip(side).start()
    for side in range(2):
        strip(side).wait()

    for s in range(6):
        after = pltpu.roll(edges[1], (LANES - 4 * s) % LANES, 1)
        before = pltpu.roll(edges[0], 4 * s, 1)
        fields[s, :, pl.ds(width, LANES)] = jnp.where(
            lane == 0, after, jnp.where(lane >= LANES - 3, before, 0.0)
        )

    def total(count):
        out = None
        for slot in range(count):
            pltpu.make_async_copy(inbox.at[slot], inbox.at[slot], in_sem.at[slot]).wait()
            out = inbox[slot] if out is None else out + inbox[slot]
        return out

    stores = [
        pltpu.make_async_copy(state.at[s], new_hbm.at[0, :, s, :], load_sem.at[s])
        for s in range(4)
    ] + [
        pltpu.make_async_copy(velocity.at[a], coupled_hbm.at[0, :, a, :], load_sem.at[4 + a])
        for a in range(2)
    ]

    def give(out):
        for a in range(2):
            for part in range(parts):
                velocity[a, :, pl.ds(part * LANES, LANES)] = out[
                    part * padded : part * padded + rows, a * LANES : (a + 1) * LANES
                ]
            stores[4 + a].start()

    def sent(count):
        for slot in range(count):
            pltpu.make_async_copy(
                outbox.at[slot], outbox.at[slot], out_sem.at[slot]
            ).wait()

    @pl.when(me != ocean)
    def _():
        derivative, stiffness = stencils()
        columns = lax.rem(lax.broadcasted_iota(jnp.int32, (padded, width), 1), 3)
        row = lax.broadcasted_iota(jnp.int32, (padded, width), 0)
        row_kind = lax.rem(row, 3)
        row_kind = jnp.where(row == 0, 3, jnp.where(row == rows - 1, 4, row_kind))
        east = fields[4, :, pl.ds(0, width)]
        north = fields[6, :, pl.ds(0, width)]
        for s in range(4):
            along_x = along_y = stiff = None
            whole = fields[s]
            centre = fields[s, :, pl.ds(0, width)]
            for k in range(7):
                step = k - 3
                shifted = whole if step == 0 else pltpu.roll(whole, (-step) % wide, 1)
                shifted = shifted[:, :width]
                first = by_kind(columns, derivative[:3, k]) * shifted
                second = by_kind(columns, stiffness[:3, k]) * shifted
                shifted = centre if step == 0 else pltpu.roll(centre, (-step) % padded, 0)
                third = by_kind(row_kind, derivative[:, k]) * shifted
                second += by_kind(row_kind, stiffness[:, k]) * shifted
                along_x = first if k == 0 else along_x + first
                along_y = third if k == 0 else along_y + third
                stiff = second if k == 0 else stiff + second
            out = centre - atmos_step * (
                2.0 * (east * along_x + north * along_y) + 4.0 * viscosity * stiff
            )
            state[s] = out[:rows]
            stores[s].start()
        give(total(5))
        sent(5)

    @pl.when(me == ocean)
    def _():
        p = fields[4]
        m = fields[5]
        m_centre = m[:, :width]
        q = fields[6, :, pl.ds(0, width)]
        m_x = m * pltpu.roll(m, wide - 1, 1)
        p_x = 0.25 * (p + pltpu.roll(p, wide - 1, 1))
        m_y = m_centre * pltpu.roll(m_centre, padded - 1, 0)
        q_y = 0.25 * (q + pltpu.roll(q, padded - 1, 0))
        base = []
        for s in range(4):
            u = fields[s]
            u_next = pltpu.roll(u, wide - 1, 1)
            flux = m_x * (p_x * (u + u_next) - diffusivity * (u_next - u))
            change = (flux - pltpu.roll(flux, 1, 1))[:, :width]
            u = u[:, :width]
            u_next = pltpu.roll(u, padded - 1, 0)
            flux = m_y * (q_y * (u + u_next) - diffusivity * (u_next - u))
            change = change + (flux - pltpu.roll(flux, 1, 0))
            other = fields[s ^ 1, :, pl.ds(0, width)]
            step = vertical_mix * (other - u) - change
            fields[s, :, pl.ds(0, width)] = u
            base.append(step)
        for s in (1, 3):
            u = fields[s, :, pl.ds(0, width)]
            state[s] = (u + m_centre * (ocean_step * base[s]))[:rows]
            stores[s].start()
        out = total(5 * ocean)
        give(out)
        for a, coef in ((0, heat_coef), (1, salt_coef)):
            s = 2 * a
            u = fields[s, :, pl.ds(0, width)]
            surface = jnp.concatenate(
                [
                    out[part * padded : (part + 1) * padded, a * LANES : (a + 1) * LANES]
                    for part in range(parts)
                ],
                1,
            )
            step = base[s] + coef * (surface - u)
            state[s] = (u + m_centre * (ocean_step * step))[:rows]
            stores[s].start()
        sent(5 * ocean)

    for copy in stores:
        copy.wait()


def by_row(array):
    return array.transpose(0, 2, 1, 3)


def local(sizes, *arrays):
    comps, tiles, rows, width, margins = sizes
    parts = width // LANES
    padded = rows + 1
    span = parts * padded
    chunks = -(-margins // CHUNK)
    roomy = -(-margins // LANES) * LANES
    arrays = tuple(by_row(array) for array in arrays[:2]) + arrays[2:]
    state, velocity = arrays[:2]
    slots = 5 * (comps - 1)
    new, coupled = pl.pallas_call(
        functools.partial(kernel, sizes),
        out_shape=(
            jax.ShapeDtypeStruct(state.shape, jnp.float32),
            jax.ShapeDtypeStruct(velocity.shape, jnp.float32),
        ),
        in_specs=[pl.BlockSpec(memory_space=pl.ANY)] * len(arrays),
        out_specs=(pl.BlockSpec(memory_space=pl.ANY),) * 2,
        scratch_shapes=[
            pltpu.VMEM((4, rows, width), jnp.float32),
            pltpu.VMEM((2, rows, width), jnp.float32),
            *[pltpu.VMEM(array.shape, array.dtype) for array in arrays[2:6]],
            pltpu.VMEM(arrays[6].shape[2:], jnp.bfloat16),
            pltpu.VMEM((span, 2 * LANES), jnp.float32),
            pltpu.VMEM((roomy, 2 * LANES), jnp.float32),
            pltpu.VMEM((roomy, 2 * LANES), jnp.float32),
            pltpu.VMEM((7, padded, width + LANES), jnp.float32),
            pltpu.VMEM((2, padded, LANES), jnp.float32),
            pltpu.VMEM((2, padded, LANES), jnp.float32),
            pltpu.VMEM((slots, span, 2 * LANES), jnp.float32),
            pltpu.VMEM((slots, span, 2 * LANES), jnp.float32),
            pltpu.SemaphoreType.DMA((10,)),
            pltpu.SemaphoreType.DMA((chunks,)),
            pltpu.SemaphoreType.DMA((slots,)),
            pltpu.SemaphoreType.DMA((slots,)),
            pltpu.SemaphoreType.DMA((2,)),
            pltpu.SemaphoreType.DMA((2,)),
        ],
        compiler_params=pltpu.CompilerParams(
            collective_id=0, has_side_effects=True, vmem_limit_bytes=56 * 2**20
        ),
    )(*arrays)
    return by_row(new), by_row(coupled)


def solution(mesh):
    comps, tiles = mesh.shape["comp"], mesh.shape["tile"]

    def whole(*arrays):
        rows, width = arrays[0].shape[2:]
        sizes = (comps, tiles, rows, width // tiles, arrays[3].shape[-1])
        placed = (
            P("comp", None, None, "tile"),
            P("comp", None, None, "tile"),
            P(None, "tile"),
            P("comp", "tile", None),
            P("comp", "tile", None),
            P("comp", "tile", None),
            P("comp", "tile", None, None, None),
        )
        return jax.shard_map(
            functools.partial(local, sizes),
            mesh=mesh,
            in_specs=placed,
            out_specs=(P("comp", None, None, "tile"), P("comp", None, None, "tile")),
            check_vma=False,
        )(*arrays)

    return whole
```

```python
import functools

import jax
import jax.numpy as jnp
import numpy as np
from jax import lax
from jax.experimental import pallas as pl
from jax.experimental.pallas import tpu as pltpu
from jax.sharding import PartitionSpec as P

MESH = pl.DeviceIdType.MESH

atmos_step = 0.02
viscosity = 0.3
ocean_step = 0.1
diffusivity = 0.2
vertical_mix = 0.5
heat_coef = 0.5
salt_coef = 0.5

LANES = 128
GROUP = 8
CHUNK = 40
OFFSETS = (0, 4, 1, 3, 2)


def gll_tables():
    nodes = np.array([-1.0, -1.0 / np.sqrt(5.0), 1.0 / np.sqrt(5.0), 1.0])
    weights = np.array([1.0 / 6.0, 5.0 / 6.0, 5.0 / 6.0, 1.0 / 6.0])
    legendre = (5.0 * nodes**3 - 3.0 * nodes) / 2.0
    deriv = np.zeros((4, 4))
    for row_node in range(4):
        for col_node in range(4):
            if row_node != col_node:
                deriv[row_node, col_node] = legendre[row_node] / (
                    legendre[col_node] * (nodes[row_node] - nodes[col_node])
                )
    deriv[0, 0] = -3.0
    deriv[3, 3] = 3.0
    return deriv, weights


def stencils():
    deriv, weights = gll_tables()
    stiff = np.einsum("k,kj,km->jm", weights, deriv, deriv)
    derivative = np.zeros((5, 7))
    stiffness = np.zeros((5, 7))
    for kind, holders in enumerate(((0, 3), (1,), (2,), (0,), (3,))):
        total = sum(weights[j] for j in holders)
        for j in holders:
            for m in range(4):
                derivative[kind, m - j + 3] += weights[j] * deriv[j, m] / total
                stiffness[kind, m - j + 3] += stiff[j, m] / total
    return derivative, stiffness


def by_kind(kinds, values):
    out = jnp.full(kinds.shape, float(values[0]), jnp.float32)
    for kind in range(1, len(values)):
        out = jnp.where(kinds == kind, float(values[kind]), out)
    return out


def kernel(
    sizes,
    state_hbm,
    velocity_hbm,
    wet_hbm,
    source_hbm,
    dest_hbm,
    block_hbm,
    weight_hbm,
    new,
    coupled,
    state,
    velocity,
    wet,
    source,
    dest,
    block,
    weight,
    payload,
    picked,
    pieces,
    fields,
    strips,
    edges,
    outbox,
    inbox,
    load_sem,
    chunk_sem,
    out_sem,
    in_sem,
    strip_sem,
    edge_sem,
):
    comps, tiles, rows, width, margins = sizes
    ocean = comps - 1
    padded = rows + 1
    parts = width // LANES
    span = parts * padded
    wide = width + LANES
    me = lax.axis_index("comp")
    tile = lax.axis_index("tile")

    def tile_at(step):
        return lax.rem(tile + step + tiles, tiles)

    def device(comp, step):
        return {"comp": comp, "tile": tile_at(step)}

    barrier = pltpu.get_barrier_semaphore()

    def greet(comp, step):
        pl.semaphore_signal(
            barrier, inc=1, device_id=device(comp, step), device_id_type=MESH
        )

    greet(me, -1)
    greet(me, 1)

    @pl.when(me == ocean)
    def _():
        for k in range(5):
            for comp in range(ocean):
                greet(comp, k - 2)

    @pl.when(me != ocean)
    def _():
        for k in range(5):
            greet(ocean, k - 2)

    loads = [
        pltpu.make_async_copy(src, dst, load_sem.at[i])
        for i, (src, dst) in enumerate(
            (
                (source_hbm, source),
                (state_hbm.at[0, :, 0, :], state.at[0]),
                (state_hbm.at[0, :, 2, :], state.at[2]),
                (dest_hbm, dest),
                (block_hbm, block),
                (state_hbm.at[0, :, 1, :], state.at[1]),
                (state_hbm.at[0, :, 3, :], state.at[3]),
                (velocity_hbm.at[0, :, 0, :], velocity.at[0]),
                (velocity_hbm.at[0, :, 1, :], velocity.at[1]),
                (wet_hbm, wet),
            )
        )
    ]
    bounds = [(low, min(low + CHUNK, margins)) for low in range(0, margins, CHUNK)]
    chunks = [
        pltpu.make_async_copy(
            weight_hbm.at[0, 0, pl.ds(low, high - low)],
            weight.at[pl.ds(low, high - low)],
            chunk_sem.at[i],
        )
        for i, (low, high) in enumerate(bounds)
    ]
    for copy in loads[:5] + chunks + loads[5:]:
        copy.start()

    payload[...] = jnp.zeros_like(payload)
    pieces[pl.ds(margins // 8 * 8, pieces.shape[0] - margins // 8 * 8), :] = jnp.zeros(
        (pieces.shape[0] - margins // 8 * 8, 2 * LANES), jnp.float32
    )
    for copy in loads[:3]:
        copy.wait()
    for a in range(2):
        for part in range(parts):
            payload[pl.ds(part * padded, rows), pl.ds(a * LANES, LANES)] = state[
                2 * a, :, pl.ds(part * LANES, LANES)
            ]

    def place_of(numbers):
        row = (numbers * 171) >> 9
        return (numbers - 3 * row) * padded + row

    slots = lax.broadcasted_iota(jnp.int32, (span, margins), 0)
    chosen = (slots == place_of(source[0])).astype(jnp.float32)
    picked[pl.ds(0, margins), :] = lax.dot_general(
        chosen.T.astype(jnp.bfloat16),
        payload[...].astype(jnp.bfloat16),
        (((1,), (0,)), ((), ())),
        preferred_element_type=jnp.float32,
    )

    for copy in loads[5:]:
        copy.wait()
    for s in range(4):
        fields[s, pl.ds(0, rows), pl.ds(0, width)] = state[s]
    fields[4, pl.ds(0, rows), pl.ds(0, width)] = velocity[0]
    fields[5, pl.ds(0, rows), pl.ds(0, width)] = wet[...].astype(jnp.float32)
    fields[6, pl.ds(0, rows), pl.ds(0, width)] = velocity[1]
    for s in range(7):
        fields[s, pl.ds(rows, 1), pl.ds(0, width)] = jnp.zeros((1, width), jnp.float32)
    lane = lax.broadcasted_iota(jnp.int32, (padded, LANES), 1)
    right_going = fields[0, :, pl.ds(width - LANES, LANES)]
    left_going = fields[0, :, pl.ds(0, LANES)]
    for s in range(1, 6):
        moved = pltpu.roll(fields[s, :, pl.ds(width - LANES, LANES)], LANES - 4 * s, 1)
        right_going = jnp.where(lane < LANES - 4 * s, moved, right_going)
        moved = pltpu.roll(fields[s, :, pl.ds(0, LANES)], 4 * s, 1)
        left_going = jnp.where(lane >= 4 * s, moved, left_going)
    strips[0] = right_going
    strips[1] = left_going

    rank = lax.rem(lax.broadcasted_iota(jnp.int32, (2 * GROUP, LANES), 0), GROUP)
    for (low, high), copy in zip(bounds, chunks):
        copy.wait()
        for first in range(low, high, GROUP):
            count = min(GROUP, high - first)
            held = jnp.concatenate(
                [picked[pl.ds(first, GROUP), pl.ds(a * LANES, LANES)] for a in range(2)], 0
            )
            spread = jnp.concatenate(
                [jnp.where(rank == i, held, 0.0).astype(jnp.bfloat16) for i in range(count)], 1
            )
            product = jnp.dot(
                spread,
                weight[pl.ds(first, count)].reshape(count * LANES, LANES),
                preferred_element_type=jnp.float32,
            )
            for a in range(2):
                pieces[pl.ds(first, count), pl.ds(a * LANES, LANES)] = product[
                    a * GROUP : a * GROUP + count
                ]

    loads[3].wait()
    loads[4].wait()
    target = dest[0]
    offset = (target & (tiles - 1)) - tile + 2
    offset = jnp.where(offset < 0, offset + tiles, offset)
    offset = jnp.where(offset >= tiles, offset - tiles, offset)
    place = place_of(block[0])
    whole = pieces[...]
    coarse = whole.astype(jnp.bfloat16)
    fine = (whole - coarse.astype(jnp.float32)).astype(jnp.bfloat16)

    def gathered(codes, low, count):
        numbers = lax.broadcasted_iota(jnp.int32, (count, margins), 0) + low
        onehot = (numbers == codes).astype(jnp.float32).astype(jnp.bfloat16)
        return jnp.dot(
            onehot, coarse[:margins], preferred_element_type=jnp.float32
        ) + jnp.dot(onehot, fine[:margins], preferred_element_type=jnp.float32)

    def message(slot, far_slot, comp, k):
        return pltpu.make_async_remote_copy(
            src_ref=outbox.at[slot],
            dst_ref=inbox.at[far_slot],
            send_sem=out_sem.at[slot],
            recv_sem=in_sem.at[far_slot],
            device_id=device(comp, k - 2),
            device_id_type=MESH,
        )

    def strip(side):
        return pltpu.make_async_remote_copy(
            src_ref=strips.at[side],
            dst_ref=edges.at[side],
            send_sem=strip_sem.at[side],
            recv_sem=edge_sem.at[side],
            device_id=device(me, 1 - 2 * side),
            device_id_type=MESH,
        )

    @pl.when(me == ocean)
    def _():
        pl.semaphore_wait(barrier, 2 + 5 * ocean)
        codes = (offset * ocean + (target >> 5)) * span + place
        for k in OFFSETS:
            out = gathered(codes, k * ocean * span, ocean * span)
            for comp in range(ocean):
                outbox[comp * 5 + k] = out[comp * span : (comp + 1) * span]
                message(comp * 5 + k, k, comp, k).start()

    @pl.when(me != ocean)
    def _():
        pl.semaphore_wait(barrier, 2 + 5)
        codes = offset * span + place
        for k in OFFSETS:
            outbox[k] = gathered(codes, k * span, span)
            message(k, me * 5 + k, ocean, k).start()

    for side in range(2):
        strip(side).start()
    for side in range(2):
        strip(side).wait()

    for s in range(6):
        after = pltpu.roll(edges[1], (LANES - 4 * s) % LANES, 1)
        before = pltpu.roll(edges[0], 4 * s, 1)
        fields[s, :, pl.ds(width, LANES)] = jnp.where(
            lane == 0, after, jnp.where(lane >= LANES - 3, before, 0.0)
        )

    def total(count):
        out = None
        for slot in range(count):
            pltpu.make_async_copy(inbox.at[slot], inbox.at[slot], in_sem.at[slot]).wait()
            out = inbox[slot] if out is None else out + inbox[slot]
        return out

    def give(out):
        for a in range(2):
            for part in range(parts):
                coupled[a, :, pl.ds(part * LANES, LANES)] = out[
                    part * padded : part * padded + rows, a * LANES : (a + 1) * LANES
                ]

    def sent(count):
        for slot in range(count):
            pltpu.make_async_copy(
                outbox.at[slot], outbox.at[slot], out_sem.at[slot]
            ).wait()

    @pl.when(me != ocean)
    def _():
        derivative, stiffness = stencils()
        columns = lax.rem(lax.broadcasted_iota(jnp.int32, (padded, width), 1), 3)
        row = lax.broadcasted_iota(jnp.int32, (padded, width), 0)
        row_kind = lax.rem(row, 3)
        row_kind = jnp.where(row == 0, 3, jnp.where(row == rows - 1, 4, row_kind))
        east = fields[4, :, pl.ds(0, width)]
        north = fields[6, :, pl.ds(0, width)]
        for s in range(4):
            along_x = along_y = stiff = None
            whole = fields[s]
            centre = fields[s, :, pl.ds(0, width)]
            for k in range(7):
                step = k - 3
                shifted = whole if step == 0 else pltpu.roll(whole, (-step) % wide, 1)
                shifted = shifted[:, :width]
                first = by_kind(columns, derivative[:3, k]) * shifted
                second = by_kind(columns, stiffness[:3, k]) * shifted
                shifted = centre if step == 0 else pltpu.roll(centre, (-step) % padded, 0)
                third = by_kind(row_kind, derivative[:, k]) * shifted
                second += by_kind(row_kind, stiffness[:, k]) * shifted
                along_x = first if k == 0 else along_x + first
                along_y = third if k == 0 else along_y + third
                stiff = second if k == 0 else stiff + second
            out = centre - atmos_step * (
                2.0 * (east * along_x + north * along_y) + 4.0 * viscosity * stiff
            )
            new[s] = out[:rows]
        give(total(5))
        sent(5)

    @pl.when(me == ocean)
    def _():
        p = fields[4]
        m = fields[5]
        m_centre = m[:, :width]
        q = fields[6, :, pl.ds(0, width)]
        m_x = m * pltpu.roll(m, wide - 1, 1)
        p_x = 0.25 * (p + pltpu.roll(p, wide - 1, 1))
        m_y = m_centre * pltpu.roll(m_centre, padded - 1, 0)
        q_y = 0.25 * (q + pltpu.roll(q, padded - 1, 0))
        base = []
        for s in range(4):
            u = fields[s]
            u_next = pltpu.roll(u, wide - 1, 1)
            flux = m_x * (p_x * (u + u_next) - diffusivity * (u_next - u))
            change = (flux - pltpu.roll(flux, 1, 1))[:, :width]
            u = u[:, :width]
            u_next = pltpu.roll(u, padded - 1, 0)
            flux = m_y * (q_y * (u + u_next) - diffusivity * (u_next - u))
            change = change + (flux - pltpu.roll(flux, 1, 0))
            other = fields[s ^ 1, :, pl.ds(0, width)]
            step = vertical_mix * (other - u) - change
            fields[s, :, pl.ds(0, width)] = u
            base.append(step)
        for s in (1, 3):
            u = fields[s, :, pl.ds(0, width)]
            new[s] = (u + m_centre * (ocean_step * base[s]))[:rows]
        out = total(5 * ocean)
        give(out)
        for a, coef in ((0, heat_coef), (1, salt_coef)):
            s = 2 * a
            u = fields[s, :, pl.ds(0, width)]
            surface = jnp.concatenate(
                [
                    out[part * padded : (part + 1) * padded, a * LANES : (a + 1) * LANES]
                    for part in range(parts)
                ],
                1,
            )
            step = base[s] + coef * (surface - u)
            new[s] = (u + m_centre * (ocean_step * step))[:rows]
        sent(5 * ocean)


def write(new_in, coupled_in, new_hbm, coupled_hbm, sem, new, coupled, load_sem):
    loads = [
        pltpu.make_async_copy(src.at[s], dst.at[s], load_sem.at[i, s])
        for i, (src, dst) in enumerate(((new_in, new), (coupled_in, coupled)))
        for s in range(src.shape[0])
    ]
    for copy in loads:
        copy.start()
    stores = [
        pltpu.make_async_copy(slabs.at[s], out.at[0, :, s, :], sem.at[i, s])
        for i, (slabs, out) in enumerate(((new, new_hbm), (coupled, coupled_hbm)))
        for s in range(slabs.shape[0])
    ]
    for load, copy in zip(loads, stores):
        load.wait()
        copy.start()
    for copy in stores:
        copy.wait()


def by_row(array):
    return array.transpose(0, 2, 1, 3)


def local(sizes, *arrays):
    comps, tiles, rows, width, margins = sizes
    parts = width // LANES
    padded = rows + 1
    span = parts * padded
    chunks = -(-margins // CHUNK)
    roomy = -(-margins // LANES) * LANES
    arrays = tuple(by_row(array) for array in arrays[:2]) + arrays[2:]
    state, velocity = arrays[:2]
    slots = 5 * (comps - 1)
    new, coupled = pl.pallas_call(
        functools.partial(kernel, sizes),
        out_shape=(
            jax.ShapeDtypeStruct((4, rows, width), jnp.float32),
            jax.ShapeDtypeStruct((2, rows, width), jnp.float32),
        ),
        in_specs=[pl.BlockSpec(memory_space=pl.ANY)] * len(arrays),
        out_specs=(pl.BlockSpec(memory_space=pltpu.VMEM),) * 2,
        scratch_shapes=[
            pltpu.VMEM((4, rows, width), jnp.float32),
            pltpu.VMEM((2, rows, width), jnp.float32),
            *[pltpu.VMEM(array.shape, array.dtype) for array in arrays[2:6]],
            pltpu.VMEM(arrays[6].shape[2:], jnp.bfloat16),
            pltpu.VMEM((span, 2 * LANES), jnp.float32),
            pltpu.VMEM((roomy, 2 * LANES), jnp.float32),
            pltpu.VMEM((roomy, 2 * LANES), jnp.float32),
            pltpu.VMEM((7, padded, width + LANES), jnp.float32),
            pltpu.VMEM((2, padded, LANES), jnp.float32),
            pltpu.VMEM((2, padded, LANES), jnp.float32),
            pltpu.VMEM((slots, span, 2 * LANES), jnp.float32),
            pltpu.VMEM((slots, span, 2 * LANES), jnp.float32),
            pltpu.SemaphoreType.DMA((10,)),
            pltpu.SemaphoreType.DMA((chunks,)),
            pltpu.SemaphoreType.DMA((slots,)),
            pltpu.SemaphoreType.DMA((slots,)),
            pltpu.SemaphoreType.DMA((2,)),
            pltpu.SemaphoreType.DMA((2,)),
        ],
        compiler_params=pltpu.CompilerParams(
            collective_id=0, has_side_effects=True, vmem_limit_bytes=56 * 2**20
        ),
    )(*arrays)
    new, coupled = pl.pallas_call(
        write,
        out_shape=(
            jax.ShapeDtypeStruct(state.shape, jnp.float32),
            jax.ShapeDtypeStruct(velocity.shape, jnp.float32),
        ),
        in_specs=[pl.BlockSpec(memory_space=pl.ANY)] * 2,
        out_specs=(pl.BlockSpec(memory_space=pl.ANY),) * 2,
        scratch_shapes=[
            pltpu.SemaphoreType.DMA((2, 4)),
            pltpu.VMEM((4, rows, width), jnp.float32),
            pltpu.VMEM((2, rows, width), jnp.float32),
            pltpu.SemaphoreType.DMA((2, 4)),
        ],
    )(new, coupled)
    return by_row(new), by_row(coupled)


def solution(mesh):
    comps, tiles = mesh.shape["comp"], mesh.shape["tile"]

    def whole(*arrays):
        rows, width = arrays[0].shape[2:]
        sizes = (comps, tiles, rows, width // tiles, arrays[3].shape[-1])
        placed = (
            P("comp", None, None, "tile"),
            P("comp", None, None, "tile"),
            P(None, "tile"),
            P("comp", "tile", None),
            P("comp", "tile", None),
            P("comp", "tile", None),
            P("comp", "tile", None, None, None),
        )
        return jax.shard_map(
            functools.partial(local, sizes),
            mesh=mesh,
            in_specs=placed,
            out_specs=(P("comp", None, None, "tile"), P("comp", None, None, "tile")),
            check_vma=False,
        )(*arrays)

    return whole
```

```python
import functools

import jax
import jax.numpy as jnp
import numpy as np
from jax import lax
from jax.experimental import pallas as pl
from jax.experimental.pallas import tpu as pltpu
from jax.sharding import PartitionSpec as P

MESH = pl.DeviceIdType.MESH

atmos_step = 0.02
viscosity = 0.3
ocean_step = 0.1
diffusivity = 0.2
vertical_mix = 0.5
heat_coef = 0.5
salt_coef = 0.5

LANES = 128
GROUP = 8
CHUNK = 40
OFFSETS = (0, 4, 1, 3, 2)


def gll_tables():
    nodes = np.array([-1.0, -1.0 / np.sqrt(5.0), 1.0 / np.sqrt(5.0), 1.0])
    weights = np.array([1.0 / 6.0, 5.0 / 6.0, 5.0 / 6.0, 1.0 / 6.0])
    legendre = (5.0 * nodes**3 - 3.0 * nodes) / 2.0
    deriv = np.zeros((4, 4))
    for row_node in range(4):
        for col_node in range(4):
            if row_node != col_node:
                deriv[row_node, col_node] = legendre[row_node] / (
                    legendre[col_node] * (nodes[row_node] - nodes[col_node])
                )
    deriv[0, 0] = -3.0
    deriv[3, 3] = 3.0
    return deriv, weights


def stencils():
    deriv, weights = gll_tables()
    stiff = np.einsum("k,kj,km->jm", weights, deriv, deriv)
    derivative = np.zeros((5, 7))
    stiffness = np.zeros((5, 7))
    for kind, holders in enumerate(((0, 3), (1,), (2,), (0,), (3,))):
        total = sum(weights[j] for j in holders)
        for j in holders:
            for m in range(4):
                derivative[kind, m - j + 3] += weights[j] * deriv[j, m] / total
                stiffness[kind, m - j + 3] += stiff[j, m] / total
    return derivative, stiffness


def by_kind(kinds, values):
    out = jnp.full(kinds.shape, float(values[0]), jnp.float32)
    for kind in range(1, len(values)):
        out = jnp.where(kinds == kind, float(values[kind]), out)
    return out


def kernel(
    sizes,
    state_hbm,
    velocity_hbm,
    wet_hbm,
    source_hbm,
    dest_hbm,
    block_hbm,
    weight_hbm,
    new,
    coupled,
    state,
    velocity,
    wet,
    source,
    dest,
    block,
    weight,
    payload,
    picked,
    pieces,
    onehot,
    fields,
    strips,
    edges,
    outbox,
    inbox,
    load_sem,
    chunk_sem,
    out_sem,
    in_sem,
    strip_sem,
    edge_sem,
):
    comps, tiles, rows, width, margins = sizes
    ocean = comps - 1
    padded = rows + 1
    parts = width // LANES
    span = parts * padded
    wide = width + LANES
    me = lax.axis_index("comp")
    tile = lax.axis_index("tile")

    def tile_at(step):
        return lax.rem(tile + step + tiles, tiles)

    def device(comp, step):
        return {"comp": comp, "tile": tile_at(step)}

    barrier = pltpu.get_barrier_semaphore()

    def greet(comp, step):
        pl.semaphore_signal(
            barrier, inc=1, device_id=device(comp, step), device_id_type=MESH
        )

    greet(me, -1)
    greet(me, 1)

    @pl.when(me == ocean)
    def _():
        for k in range(5):
            for comp in range(ocean):
                greet(comp, k - 2)

    @pl.when(me != ocean)
    def _():
        for k in range(5):
            greet(ocean, k - 2)

    loads = [
        pltpu.make_async_copy(src, dst, load_sem.at[i])
        for i, (src, dst) in enumerate(
            (
                (source_hbm, source),
                (state_hbm.at[0, :, 0, :], state.at[0]),
                (state_hbm.at[0, :, 2, :], state.at[2]),
                (dest_hbm, dest),
                (block_hbm, block),
                (state_hbm.at[0, :, 1, :], state.at[1]),
                (state_hbm.at[0, :, 3, :], state.at[3]),
                (velocity_hbm.at[0, :, 0, :], velocity.at[0]),
                (velocity_hbm.at[0, :, 1, :], velocity.at[1]),
                (wet_hbm, wet),
            )
        )
    ]
    bounds = [(low, min(low + CHUNK, margins)) for low in range(0, margins, CHUNK)]
    chunks = [
        pltpu.make_async_copy(
            weight_hbm.at[0, 0, pl.ds(low, high - low)],
            weight.at[pl.ds(low, high - low)],
            chunk_sem.at[i],
        )
        for i, (low, high) in enumerate(bounds)
    ]
    for copy in loads[:5] + chunks + loads[5:]:
        copy.start()

    payload[...] = jnp.zeros_like(payload)
    pieces[pl.ds(margins // 8 * 8, pieces.shape[0] - margins // 8 * 8), :] = jnp.zeros(
        (pieces.shape[0] - margins // 8 * 8, 2 * LANES), jnp.float32
    )
    for copy in loads[:3]:
        copy.wait()
    for a in range(2):
        for part in range(parts):
            payload[pl.ds(part * padded, rows), pl.ds(a * LANES, LANES)] = state[
                2 * a, :, pl.ds(part * LANES, LANES)
            ]

    def place_of(numbers):
        row = (numbers * 171) >> 9
        return (numbers - 3 * row) * padded + row

    slots = lax.broadcasted_iota(jnp.int32, (span, margins), 0)
    chosen = (slots == place_of(source[0])).astype(jnp.float32)
    picked[pl.ds(0, margins), :] = lax.dot_general(
        chosen.T.astype(jnp.bfloat16),
        payload[...].astype(jnp.bfloat16),
        (((1,), (0,)), ((), ())),
        preferred_element_type=jnp.float32,
    )

    for copy in loads[5:]:
        copy.wait()
    for s in range(4):
        fields[s, pl.ds(0, rows), pl.ds(0, width)] = state[s]
    fields[4, pl.ds(0, rows), pl.ds(0, width)] = velocity[0]
    fields[5, pl.ds(0, rows), pl.ds(0, width)] = wet[...].astype(jnp.float32)
    fields[6, pl.ds(0, rows), pl.ds(0, width)] = velocity[1]
    for s in range(7):
        fields[s, pl.ds(rows, 1), pl.ds(0, width)] = jnp.zeros((1, width), jnp.float32)
    lane = lax.broadcasted_iota(jnp.int32, (padded, LANES), 1)
    right_going = fields[0, :, pl.ds(width - LANES, LANES)]
    left_going = fields[0, :, pl.ds(0, LANES)]
    for s in range(1, 6):
        moved = pltpu.roll(fields[s, :, pl.ds(width - LANES, LANES)], LANES - 4 * s, 1)
        right_going = jnp.where(lane < LANES - 4 * s, moved, right_going)
        moved = pltpu.roll(fields[s, :, pl.ds(0, LANES)], 4 * s, 1)
        left_going = jnp.where(lane >= 4 * s, moved, left_going)
    strips[0] = right_going
    strips[1] = left_going

    loads[3].wait()
    loads[4].wait()
    target = dest[0]
    offset = (target & (tiles - 1)) - tile + 2
    offset = jnp.where(offset < 0, offset + tiles, offset)
    offset = jnp.where(offset >= tiles, offset - tiles, offset)
    place = place_of(block[0])
    codes = offset * span + place
    codes = jnp.where(me == ocean, (target >> 5) * (5 * span) + codes, codes)
    numbers = lax.broadcasted_iota(jnp.int32, (span, margins), 0)

    def mark(slot):
        onehot[pl.ds(slot * span, span), pl.ds(0, margins)] = (
            (numbers == codes - slot * span).astype(jnp.float32).astype(jnp.bfloat16)
        )

    onehot[...] = jnp.zeros_like(onehot)
    for slot in range(5):
        mark(slot)

    @pl.when(me == ocean)
    def _():
        for slot in range(5, 5 * ocean):
            mark(slot)

    rank = lax.rem(lax.broadcasted_iota(jnp.int32, (2 * GROUP, LANES), 0), GROUP)
    for (low, high), copy in zip(bounds, chunks):
        copy.wait()
        for first in range(low, high, GROUP):
            count = min(GROUP, high - first)
            held = jnp.concatenate(
                [picked[pl.ds(first, GROUP), pl.ds(a * LANES, LANES)] for a in range(2)], 0
            )
            spread = jnp.concatenate(
                [jnp.where(rank == i, held, 0.0).astype(jnp.bfloat16) for i in range(count)], 1
            )
            product = jnp.dot(
                spread,
                weight[pl.ds(first, count)].reshape(count * LANES, LANES),
                preferred_element_type=jnp.float32,
            )
            for a in range(2):
                pieces[pl.ds(first, count), pl.ds(a * LANES, LANES)] = product[
                    a * GROUP : a * GROUP + count
                ]

    whole = pieces[...]
    coarse = whole.astype(jnp.bfloat16)
    fine = (whole - coarse.astype(jnp.float32)).astype(jnp.bfloat16)

    def gathered(low, count):
        held = onehot[pl.ds(low, count), :]
        return jnp.dot(held, coarse, preferred_element_type=jnp.float32) + jnp.dot(
            held, fine, preferred_element_type=jnp.float32
        )

    def message(slot, far_slot, comp, k):
        return pltpu.make_async_remote_copy(
            src_ref=outbox.at[slot],
            dst_ref=inbox.at[far_slot],
            send_sem=out_sem.at[slot],
            recv_sem=in_sem.at[far_slot],
            device_id=device(comp, k - 2),
            device_id_type=MESH,
        )

    def strip(side):
        return pltpu.make_async_remote_copy(
            src_ref=strips.at[side],
            dst_ref=edges.at[side],
            send_sem=strip_sem.at[side],
            recv_sem=edge_sem.at[side],
            device_id=device(me, 1 - 2 * side),
            device_id_type=MESH,
        )

    @pl.when(me == ocean)
    def _():
        pl.semaphore_wait(barrier, 2 + 5 * ocean)
        order = [(comp, k) for k in OFFSETS for comp in range(ocean - 1)]
        for comp, k in order + [(ocean - 1, k) for k in OFFSETS]:
            slot = comp * 5 + k
            outbox[slot] = gathered(slot * span, span)
            message(slot, k, comp, k).start()

    @pl.when(me != ocean)
    def _():
        pl.semaphore_wait(barrier, 2 + 5)
        for k in OFFSETS:
            outbox[k] = gathered(k * span, span)
            message(k, me * 5 + k, ocean, k).start()

    for side in range(2):
        strip(side).start()
    for side in range(2):
        strip(side).wait()

    for s in range(6):
        after = pltpu.roll(edges[1], (LANES - 4 * s) % LANES, 1)
        before = pltpu.roll(edges[0], 4 * s, 1)
        fields[s, :, pl.ds(width, LANES)] = jnp.where(
            lane == 0, after, jnp.where(lane >= LANES - 3, before, 0.0)
        )

    def total(count):
        out = None
        for slot in range(count):
            pltpu.make_async_copy(inbox.at[slot], inbox.at[slot], in_sem.at[slot]).wait()
            out = inbox[slot] if out is None else out + inbox[slot]
        return out

    def give(out):
        for a in range(2):
            for part in range(parts):
                coupled[a, :, pl.ds(part * LANES, LANES)] = out[
                    part * padded : part * padded + rows, a * LANES : (a + 1) * LANES
                ]

    def sent(count):
        for slot in range(count):
            pltpu.make_async_copy(
                outbox.at[slot], outbox.at[slot], out_sem.at[slot]
            ).wait()

    @pl.when(me != ocean)
    def _():
        derivative, stiffness = stencils()
        columns = lax.rem(lax.broadcasted_iota(jnp.int32, (padded, width), 1), 3)
        row = lax.broadcasted_iota(jnp.int32, (padded, width), 0)
        row_kind = lax.rem(row, 3)
        row_kind = jnp.where(row == 0, 3, jnp.where(row == rows - 1, 4, row_kind))
        east = fields[4, :, pl.ds(0, width)]
        north = fields[6, :, pl.ds(0, width)]
        for s in range(4):
            along_x = along_y = stiff = None
            whole = fields[s]
            centre = fields[s, :, pl.ds(0, width)]
            for k in range(7):
                step = k - 3
                shifted = whole if step == 0 else pltpu.roll(whole, (-step) % wide, 1)
                shifted = shifted[:, :width]
                first = by_kind(columns, derivative[:3, k]) * shifted
                second = by_kind(columns, stiffness[:3, k]) * shifted
                shifted = centre if step == 0 else pltpu.roll(centre, (-step) % padded, 0)
                third = by_kind(row_kind, derivative[:, k]) * shifted
                second += by_kind(row_kind, stiffness[:, k]) * shifted
                along_x = first if k == 0 else along_x + first
                along_y = third if k == 0 else along_y + third
                stiff = second if k == 0 else stiff + second
            out = centre - atmos_step * (
                2.0 * (east * along_x + north * along_y) + 4.0 * viscosity * stiff
            )
            new[s] = out[:rows]
        give(total(5))
        sent(5)

    @pl.when(me == ocean)
    def _():
        p = fields[4]
        m = fields[5]
        m_centre = m[:, :width]
        q = fields[6, :, pl.ds(0, width)]
        m_x = m * pltpu.roll(m, wide - 1, 1)
        p_x = 0.25 * (p + pltpu.roll(p, wide - 1, 1))
        m_y = m_centre * pltpu.roll(m_centre, padded - 1, 0)
        q_y = 0.25 * (q + pltpu.roll(q, padded - 1, 0))
        base = []
        for s in range(4):
            u = fields[s]
            u_next = pltpu.roll(u, wide - 1, 1)
            flux = m_x * (p_x * (u + u_next) - diffusivity * (u_next - u))
            change = (flux - pltpu.roll(flux, 1, 1))[:, :width]
            u = u[:, :width]
            u_next = pltpu.roll(u, padded - 1, 0)
            flux = m_y * (q_y * (u + u_next) - diffusivity * (u_next - u))
            change = change + (flux - pltpu.roll(flux, 1, 0))
            other = fields[s ^ 1, :, pl.ds(0, width)]
            step = vertical_mix * (other - u) - change
            fields[s, :, pl.ds(0, width)] = u
            base.append(step)
        for s in (1, 3):
            u = fields[s, :, pl.ds(0, width)]
            new[s] = (u + m_centre * (ocean_step * base[s]))[:rows]
        out = total(5 * ocean)
        give(out)
        for a, coef in ((0, heat_coef), (1, salt_coef)):
            s = 2 * a
            u = fields[s, :, pl.ds(0, width)]
            surface = jnp.concatenate(
                [
                    out[part * padded : (part + 1) * padded, a * LANES : (a + 1) * LANES]
                    for part in range(parts)
                ],
                1,
            )
            step = base[s] + coef * (surface - u)
            new[s] = (u + m_centre * (ocean_step * step))[:rows]
        sent(5 * ocean)


def write(new, coupled, new_hbm, coupled_hbm, sem):
    stores = [
        pltpu.make_async_copy(slabs.at[s], out.at[0, :, s, :], sem.at[i, s])
        for i, (slabs, out) in enumerate(((new, new_hbm), (coupled, coupled_hbm)))
        for s in range(slabs.shape[0])
    ]
    for copy in stores:
        copy.start()
    for copy in stores:
        copy.wait()


def by_row(array):
    return array.transpose(0, 2, 1, 3)


def local(sizes, *arrays):
    comps, tiles, rows, width, margins = sizes
    parts = width // LANES
    padded = rows + 1
    span = parts * padded
    chunks = -(-margins // CHUNK)
    roomy = -(-margins // LANES) * LANES
    arrays = tuple(by_row(array) for array in arrays[:2]) + arrays[2:]
    state, velocity = arrays[:2]
    slots = 5 * (comps - 1)
    new, coupled = pl.pallas_call(
        functools.partial(kernel, sizes),
        out_shape=(
            pltpu.VMEM((4, rows, width), jnp.float32),
            pltpu.VMEM((2, rows, width), jnp.float32),
        ),
        in_specs=[pl.BlockSpec(memory_space=pl.ANY)] * len(arrays),
        out_specs=(pl.BlockSpec(memory_space=pltpu.VMEM),) * 2,
        scratch_shapes=[
            pltpu.VMEM((4, rows, width), jnp.float32),
            pltpu.VMEM((2, rows, width), jnp.float32),
            *[pltpu.VMEM(array.shape, array.dtype) for array in arrays[2:6]],
            pltpu.VMEM(arrays[6].shape[2:], jnp.bfloat16),
            pltpu.VMEM((span, 2 * LANES), jnp.float32),
            pltpu.VMEM((roomy, 2 * LANES), jnp.float32),
            pltpu.VMEM((roomy, 2 * LANES), jnp.float32),
            pltpu.VMEM((slots * span, roomy), jnp.bfloat16),
            pltpu.VMEM((7, padded, width + LANES), jnp.float32),
            pltpu.VMEM((2, padded, LANES), jnp.float32),
            pltpu.VMEM((2, padded, LANES), jnp.float32),
            pltpu.VMEM((slots, span, 2 * LANES), jnp.float32),
            pltpu.VMEM((slots, span, 2 * LANES), jnp.float32),
            pltpu.SemaphoreType.DMA((10,)),
            pltpu.SemaphoreType.DMA((chunks,)),
            pltpu.SemaphoreType.DMA((slots,)),
            pltpu.SemaphoreType.DMA((slots,)),
            pltpu.SemaphoreType.DMA((2,)),
            pltpu.SemaphoreType.DMA((2,)),
        ],
        compiler_params=pltpu.CompilerParams(
            collective_id=0, has_side_effects=True, vmem_limit_bytes=56 * 2**20
        ),
    )(*arrays)
    new, coupled = pl.pallas_call(
        write,
        out_shape=(
            jax.ShapeDtypeStruct(state.shape, jnp.float32),
            jax.ShapeDtypeStruct(velocity.shape, jnp.float32),
        ),
        in_specs=[pl.BlockSpec(memory_space=pltpu.VMEM)] * 2,
        out_specs=(pl.BlockSpec(memory_space=pl.ANY),) * 2,
        scratch_shapes=[pltpu.SemaphoreType.DMA((2, 4))],
        compiler_params=pltpu.CompilerParams(vmem_limit_bytes=2**20),
    )(new, coupled)
    return by_row(new), by_row(coupled)


def solution(mesh):
    comps, tiles = mesh.shape["comp"], mesh.shape["tile"]

    def whole(*arrays):
        rows, width = arrays[0].shape[2:]
        sizes = (comps, tiles, rows, width // tiles, arrays[3].shape[-1])
        placed = (
            P("comp", None, None, "tile"),
            P("comp", None, None, "tile"),
            P(None, "tile"),
            P("comp", "tile", None),
            P("comp", "tile", None),
            P("comp", "tile", None),
            P("comp", "tile", None, None, None),
        )
        return jax.shard_map(
            functools.partial(local, sizes),
            mesh=mesh,
            in_specs=placed,
            out_specs=(P("comp", None, None, "tile"), P("comp", None, None, "tile")),
            check_vma=False,
        )(*arrays)

    return whole
```

```python
import functools

import jax
import jax.numpy as jnp
import numpy as np
from jax import lax
from jax.experimental import pallas as pl
from jax.experimental.pallas import tpu as pltpu
from jax.sharding import PartitionSpec as P

MESH = pl.DeviceIdType.MESH

atmos_step = 0.02
viscosity = 0.3
ocean_step = 0.1
diffusivity = 0.2
vertical_mix = 0.5
heat_coef = 0.5
salt_coef = 0.5

LANES = 128
GROUP = 8
CHUNK = 40
OFFSETS = (0, 4, 1, 3, 2)


def gll_tables():
    nodes = np.array([-1.0, -1.0 / np.sqrt(5.0), 1.0 / np.sqrt(5.0), 1.0])
    weights = np.array([1.0 / 6.0, 5.0 / 6.0, 5.0 / 6.0, 1.0 / 6.0])
    legendre = (5.0 * nodes**3 - 3.0 * nodes) / 2.0
    deriv = np.zeros((4, 4))
    for row_node in range(4):
        for col_node in range(4):
            if row_node != col_node:
                deriv[row_node, col_node] = legendre[row_node] / (
                    legendre[col_node] * (nodes[row_node] - nodes[col_node])
                )
    deriv[0, 0] = -3.0
    deriv[3, 3] = 3.0
    return deriv, weights


def stencils():
    deriv, weights = gll_tables()
    stiff = np.einsum("k,kj,km->jm", weights, deriv, deriv)
    derivative = np.zeros((5, 7))
    stiffness = np.zeros((5, 7))
    for kind, holders in enumerate(((0, 3), (1,), (2,), (0,), (3,))):
        total = sum(weights[j] for j in holders)
        for j in holders:
            for m in range(4):
                derivative[kind, m - j + 3] += weights[j] * deriv[j, m] / total
                stiffness[kind, m - j + 3] += stiff[j, m] / total
    return derivative, stiffness


def by_kind(kinds, values):
    out = jnp.full(kinds.shape, float(values[0]), jnp.float32)
    for kind in range(1, len(values)):
        out = jnp.where(kinds == kind, float(values[kind]), out)
    return out


def kernel(
    sizes,
    state_hbm,
    velocity_hbm,
    wet_hbm,
    source_hbm,
    dest_hbm,
    block_hbm,
    weight_hbm,
    new,
    coupled,
    state,
    velocity,
    wet,
    source,
    dest,
    block,
    weight,
    payload,
    picked,
    pieces,
    onehot,
    fields,
    strips,
    edges,
    outbox,
    inbox,
    load_sem,
    chunk_sem,
    out_sem,
    in_sem,
    strip_sem,
    edge_sem,
):
    comps, tiles, rows, width, margins = sizes
    ocean = comps - 1
    padded = rows + 1
    parts = width // LANES
    span = parts * padded
    wide = width + LANES
    me = lax.axis_index("comp")
    tile = lax.axis_index("tile")

    def tile_at(step):
        return lax.rem(tile + step + tiles, tiles)

    def device(comp, step):
        return {"comp": comp, "tile": tile_at(step)}

    barrier = pltpu.get_barrier_semaphore()

    def greet(comp, step):
        pl.semaphore_signal(
            barrier, inc=1, device_id=device(comp, step), device_id_type=MESH
        )

    greet(me, -1)
    greet(me, 1)

    @pl.when(me == ocean)
    def _():
        for k in range(5):
            for comp in range(ocean):
                greet(comp, k - 2)

    @pl.when(me != ocean)
    def _():
        for k in range(5):
            greet(ocean, k - 2)

    loads = [
        pltpu.make_async_copy(src, dst, load_sem.at[i])
        for i, (src, dst) in enumerate(
            (
                (source_hbm, source),
                (state_hbm.at[0, :, 0, :], state.at[0]),
                (state_hbm.at[0, :, 2, :], state.at[2]),
                (dest_hbm, dest),
                (block_hbm, block),
                (state_hbm.at[0, :, 1, :], state.at[1]),
                (state_hbm.at[0, :, 3, :], state.at[3]),
                (velocity_hbm.at[0, :, 0, :], velocity.at[0]),
                (velocity_hbm.at[0, :, 1, :], velocity.at[1]),
                (wet_hbm, wet),
            )
        )
    ]
    bounds = [(low, min(low + CHUNK, margins)) for low in range(0, margins, CHUNK)]
    chunks = [
        pltpu.make_async_copy(
            weight_hbm.at[0, 0, pl.ds(low, high - low)],
            weight.at[pl.ds(low, high - low)],
            chunk_sem.at[i],
        )
        for i, (low, high) in enumerate(bounds)
    ]
    for copy in loads + chunks:
        copy.start()

    payload[...] = jnp.zeros_like(payload)
    pieces[pl.ds(margins // 8 * 8, pieces.shape[0] - margins // 8 * 8), :] = jnp.zeros(
        (pieces.shape[0] - margins // 8 * 8, 2 * LANES), jnp.float32
    )
    for copy in loads[:3]:
        copy.wait()
    for a in range(2):
        for part in range(parts):
            payload[pl.ds(part * padded, rows), pl.ds(a * LANES, LANES)] = state[
                2 * a, :, pl.ds(part * LANES, LANES)
            ]

    def place_of(numbers):
        row = (numbers * 171) >> 9
        return (numbers - 3 * row) * padded + row

    slots = lax.broadcasted_iota(jnp.int32, (span, margins), 0)
    chosen = (slots == place_of(source[0])).astype(jnp.float32)
    picked[pl.ds(0, margins), :] = lax.dot_general(
        chosen.T.astype(jnp.bfloat16),
        payload[...].astype(jnp.bfloat16),
        (((1,), (0,)), ((), ())),
        preferred_element_type=jnp.float32,
    )

    loads[3].wait()
    loads[4].wait()
    target = dest[0]
    offset = (target & (tiles - 1)) - tile + 2
    offset = jnp.where(offset < 0, offset + tiles, offset)
    offset = jnp.where(offset >= tiles, offset - tiles, offset)
    place = place_of(block[0])
    codes = offset * span + place
    codes = jnp.where(me == ocean, (target >> 5) * (5 * span) + codes, codes)
    numbers = lax.broadcasted_iota(jnp.int32, (span, margins), 0)

    def mark(slot):
        onehot[pl.ds(slot * span, span), pl.ds(0, margins)] = (
            (numbers == codes - slot * span).astype(jnp.float32).astype(jnp.bfloat16)
        )

    lane = lax.broadcasted_iota(jnp.int32, (padded, LANES), 1)

    def take_fields():
        for copy in loads[5:]:
            copy.wait()
        for s in range(4):
            fields[s, pl.ds(0, rows), pl.ds(0, width)] = state[s]
        fields[4, pl.ds(0, rows), pl.ds(0, width)] = velocity[0]
        fields[5, pl.ds(0, rows), pl.ds(0, width)] = wet[...].astype(jnp.float32)
        fields[6, pl.ds(0, rows), pl.ds(0, width)] = velocity[1]
        for s in range(7):
            fields[s, pl.ds(rows, 1), pl.ds(0, width)] = jnp.zeros((1, width), jnp.float32)
        right_going = fields[0, :, pl.ds(width - LANES, LANES)]
        left_going = fields[0, :, pl.ds(0, LANES)]
        for s in range(1, 6):
            moved = pltpu.roll(fields[s, :, pl.ds(width - LANES, LANES)], LANES - 4 * s, 1)
            right_going = jnp.where(lane < LANES - 4 * s, moved, right_going)
            moved = pltpu.roll(fields[s, :, pl.ds(0, LANES)], 4 * s, 1)
            left_going = jnp.where(lane >= 4 * s, moved, left_going)
        strips[0] = right_going
        strips[1] = left_going

    rank = lax.rem(lax.broadcasted_iota(jnp.int32, (2 * GROUP, LANES), 0), GROUP)
    onehot[...] = jnp.zeros_like(onehot)
    per_chunk = -(-5 * ocean // (len(bounds) - 2))
    for i, ((low, high), copy) in enumerate(zip(bounds, chunks)):
        copy.wait()
        for slot in range(i * per_chunk, min((i + 1) * per_chunk, 5 * ocean)):
            mark(slot)
        if i == len(bounds) - 2:
            take_fields()
        for first in range(low, high, GROUP):
            count = min(GROUP, high - first)
            held = jnp.concatenate(
                [picked[pl.ds(first, GROUP), pl.ds(a * LANES, LANES)] for a in range(2)], 0
            )
            spread = jnp.concatenate(
                [jnp.where(rank == i, held, 0.0).astype(jnp.bfloat16) for i in range(count)], 1
            )
            product = jnp.dot(
                spread,
                weight[pl.ds(first, count)].reshape(count * LANES, LANES),
                preferred_element_type=jnp.float32,
            )
            for a in range(2):
                pieces[pl.ds(first, count), pl.ds(a * LANES, LANES)] = product[
                    a * GROUP : a * GROUP + count
                ]

    whole = pieces[...]
    coarse = whole.astype(jnp.bfloat16)
    fine = (whole - coarse.astype(jnp.float32)).astype(jnp.bfloat16)

    def gathered(low, count):
        held = onehot[pl.ds(low, count), :]
        return jnp.dot(held, coarse, preferred_element_type=jnp.float32) + jnp.dot(
            held, fine, preferred_element_type=jnp.float32
        )

    def message(slot, far_slot, comp, k):
        return pltpu.make_async_remote_copy(
            src_ref=outbox.at[slot],
            dst_ref=inbox.at[far_slot],
            send_sem=out_sem.at[slot],
            recv_sem=in_sem.at[far_slot],
            device_id=device(comp, k - 2),
            device_id_type=MESH,
        )

    def strip(side):
        return pltpu.make_async_remote_copy(
            src_ref=strips.at[side],
            dst_ref=edges.at[side],
            send_sem=strip_sem.at[side],
            recv_sem=edge_sem.at[side],
            device_id=device(me, 1 - 2 * side),
            device_id_type=MESH,
        )

    @pl.when(me == ocean)
    def _():
        pl.semaphore_wait(barrier, 2 + 5 * ocean)
        for side in range(2):
            strip(side).start()
        order = [(comp, k) for k in OFFSETS for comp in reversed(range(ocean - 1))]
        for comp, k in order + [(ocean - 1, k) for k in OFFSETS]:
            slot = comp * 5 + k
            outbox[slot] = gathered(slot * span, span)
            message(slot, k, comp, k).start()

    @pl.when(me != ocean)
    def _():
        pl.semaphore_wait(barrier, 2 + 5)
        for side in range(2):
            strip(side).start()
        for k in OFFSETS:
            outbox[k] = gathered(k * span, span)
            message(k, me * 5 + k, ocean, k).start()

    for side in range(2):
        strip(side).wait()

    for s in range(6):
        after = pltpu.roll(edges[1], (LANES - 4 * s) % LANES, 1)
        before = pltpu.roll(edges[0], 4 * s, 1)
        fields[s, :, pl.ds(width, LANES)] = jnp.where(
            lane == 0, after, jnp.where(lane >= LANES - 3, before, 0.0)
        )

    def total(count):
        out = None
        for slot in [comp * 5 + k for k in OFFSETS for comp in range(count // 5)]:
            pltpu.make_async_copy(inbox.at[slot], inbox.at[slot], in_sem.at[slot]).wait()
            out = inbox[slot] if out is None else out + inbox[slot]
        return out

    def give(out):
        for a in range(2):
            for part in range(parts):
                coupled[a, :, pl.ds(part * LANES, LANES)] = out[
                    part * padded : part * padded + rows, a * LANES : (a + 1) * LANES
                ]

    def sent(count):
        for slot in range(count):
            pltpu.make_async_copy(
                outbox.at[slot], outbox.at[slot], out_sem.at[slot]
            ).wait()

    @pl.when(me != ocean)
    def _():
        derivative, stiffness = stencils()
        columns = lax.rem(lax.broadcasted_iota(jnp.int32, (padded, width), 1), 3)
        row = lax.broadcasted_iota(jnp.int32, (padded, width), 0)
        row_kind = lax.rem(row, 3)
        row_kind = jnp.where(row == 0, 3, jnp.where(row == rows - 1, 4, row_kind))
        east = fields[4, :, pl.ds(0, width)]
        north = fields[6, :, pl.ds(0, width)]
        for s in range(4):
            along_x = along_y = stiff = None
            whole = fields[s]
            centre = fields[s, :, pl.ds(0, width)]
            for k in range(7):
                step = k - 3
                shifted = whole if step == 0 else pltpu.roll(whole, (-step) % wide, 1)
                shifted = shifted[:, :width]
                first = by_kind(columns, derivative[:3, k]) * shifted
                second = by_kind(columns, stiffness[:3, k]) * shifted
                shifted = centre if step == 0 else pltpu.roll(centre, (-step) % padded, 0)
                third = by_kind(row_kind, derivative[:, k]) * shifted
                second += by_kind(row_kind, stiffness[:, k]) * shifted
                along_x = first if k == 0 else along_x + first
                along_y = third if k == 0 else along_y + third
                stiff = second if k == 0 else stiff + second
            out = centre - atmos_step * (
                2.0 * (east * along_x + north * along_y) + 4.0 * viscosity * stiff
            )
            new[s] = out[:rows]
        give(total(5))
        sent(5)

    @pl.when(me == ocean)
    def _():
        p = fields[4]
        m = fields[5]
        m_centre = m[:, :width]
        q = fields[6, :, pl.ds(0, width)]
        m_x = m * pltpu.roll(m, wide - 1, 1)
        p_x = 0.25 * (p + pltpu.roll(p, wide - 1, 1))
        m_y = m_centre * pltpu.roll(m_centre, padded - 1, 0)
        q_y = 0.25 * (q + pltpu.roll(q, padded - 1, 0))
        base = []
        for s in range(4):
            u = fields[s]
            u_next = pltpu.roll(u, wide - 1, 1)
            flux = m_x * (p_x * (u + u_next) - diffusivity * (u_next - u))
            change = (flux - pltpu.roll(flux, 1, 1))[:, :width]
            u = u[:, :width]
            u_next = pltpu.roll(u, padded - 1, 0)
            flux = m_y * (q_y * (u + u_next) - diffusivity * (u_next - u))
            change = change + (flux - pltpu.roll(flux, 1, 0))
            other = fields[s ^ 1, :, pl.ds(0, width)]
            step = vertical_mix * (other - u) - change
            fields[s, :, pl.ds(0, width)] = u
            base.append(step)
        for s in (1, 3):
            u = fields[s, :, pl.ds(0, width)]
            new[s] = (u + m_centre * (ocean_step * base[s]))[:rows]
        out = total(5 * ocean)
        give(out)
        for a, coef in ((0, heat_coef), (1, salt_coef)):
            s = 2 * a
            u = fields[s, :, pl.ds(0, width)]
            surface = jnp.concatenate(
                [
                    out[part * padded : (part + 1) * padded, a * LANES : (a + 1) * LANES]
                    for part in range(parts)
                ],
                1,
            )
            step = base[s] + coef * (surface - u)
            new[s] = (u + m_centre * (ocean_step * step))[:rows]
        sent(5 * ocean)


def write(new, coupled, new_hbm, coupled_hbm, sem):
    stores = [
        pltpu.make_async_copy(slabs.at[s], out.at[0, :, s, :], sem.at[i, s])
        for i, (slabs, out) in enumerate(((new, new_hbm), (coupled, coupled_hbm)))
        for s in range(slabs.shape[0])
    ]
    for copy in stores:
        copy.start()
    for copy in stores:
        copy.wait()


def by_row(array):
    return array.transpose(0, 2, 1, 3)


def local(sizes, *arrays):
    comps, tiles, rows, width, margins = sizes
    parts = width // LANES
    padded = rows + 1
    span = parts * padded
    chunks = -(-margins // CHUNK)
    roomy = -(-margins // LANES) * LANES
    arrays = tuple(by_row(array) for array in arrays[:2]) + arrays[2:]
    state, velocity = arrays[:2]
    slots = 5 * (comps - 1)
    new, coupled = pl.pallas_call(
        functools.partial(kernel, sizes),
        out_shape=(
            pltpu.VMEM((4, rows, width), jnp.float32),
            pltpu.VMEM((2, rows, width), jnp.float32),
        ),
        in_specs=[pl.BlockSpec(memory_space=pl.ANY)] * len(arrays),
        out_specs=(pl.BlockSpec(memory_space=pltpu.VMEM),) * 2,
        scratch_shapes=[
            pltpu.VMEM((4, rows, width), jnp.float32),
            pltpu.VMEM((2, rows, width), jnp.float32),
            *[pltpu.VMEM(array.shape, array.dtype) for array in arrays[2:6]],
            pltpu.VMEM(arrays[6].shape[2:], jnp.bfloat16),
            pltpu.VMEM((span, 2 * LANES), jnp.float32),
            pltpu.VMEM((roomy, 2 * LANES), jnp.float32),
            pltpu.VMEM((roomy, 2 * LANES), jnp.float32),
            pltpu.VMEM((slots * span, roomy), jnp.bfloat16),
            pltpu.VMEM((7, padded, width + LANES), jnp.float32),
            pltpu.VMEM((2, padded, LANES), jnp.float32),
            pltpu.VMEM((2, padded, LANES), jnp.float32),
            pltpu.VMEM((slots, span, 2 * LANES), jnp.float32),
            pltpu.VMEM((slots, span, 2 * LANES), jnp.float32),
            pltpu.SemaphoreType.DMA((10,)),
            pltpu.SemaphoreType.DMA((chunks,)),
            pltpu.SemaphoreType.DMA((slots,)),
            pltpu.SemaphoreType.DMA((slots,)),
            pltpu.SemaphoreType.DMA((2,)),
            pltpu.SemaphoreType.DMA((2,)),
        ],
        compiler_params=pltpu.CompilerParams(
            collective_id=0, has_side_effects=True, vmem_limit_bytes=56 * 2**20
        ),
    )(*arrays)
    new, coupled = pl.pallas_call(
        write,
        out_shape=(
            jax.ShapeDtypeStruct(state.shape, jnp.float32),
            jax.ShapeDtypeStruct(velocity.shape, jnp.float32),
        ),
        in_specs=[pl.BlockSpec(memory_space=pltpu.VMEM)] * 2,
        out_specs=(pl.BlockSpec(memory_space=pl.ANY),) * 2,
        scratch_shapes=[pltpu.SemaphoreType.DMA((2, 4))],
        compiler_params=pltpu.CompilerParams(vmem_limit_bytes=2**20),
    )(new, coupled)
    return by_row(new), by_row(coupled)


def solution(mesh):
    comps, tiles = mesh.shape["comp"], mesh.shape["tile"]

    def whole(*arrays):
        rows, width = arrays[0].shape[2:]
        sizes = (comps, tiles, rows, width // tiles, arrays[3].shape[-1])
        placed = (
            P("comp", None, None, "tile"),
            P("comp", None, None, "tile"),
            P(None, "tile"),
            P("comp", "tile", None),
            P("comp", "tile", None),
            P("comp", "tile", None),
            P("comp", "tile", None, None, None),
        )
        return jax.shard_map(
            functools.partial(local, sizes),
            mesh=mesh,
            in_specs=placed,
            out_specs=(P("comp", None, None, "tile"), P("comp", None, None, "tile")),
            check_vma=False,
        )(*arrays)

    return whole
```

```python
import functools

import jax
import jax.numpy as jnp
import numpy as np
from jax import lax
from jax.experimental import pallas as pl
from jax.experimental.pallas import tpu as pltpu
from jax.sharding import PartitionSpec as P

MESH = pl.DeviceIdType.MESH

atmos_step = 0.02
viscosity = 0.3
ocean_step = 0.1
diffusivity = 0.2
vertical_mix = 0.5
heat_coef = 0.5
salt_coef = 0.5

LANES = 128
GROUP = 8
CHUNK = 40
OFFSETS = (0, 3, 1, 4, 2)


def gll_tables():
    nodes = np.array([-1.0, -1.0 / np.sqrt(5.0), 1.0 / np.sqrt(5.0), 1.0])
    weights = np.array([1.0 / 6.0, 5.0 / 6.0, 5.0 / 6.0, 1.0 / 6.0])
    legendre = (5.0 * nodes**3 - 3.0 * nodes) / 2.0
    deriv = np.zeros((4, 4))
    for row_node in range(4):
        for col_node in range(4):
            if row_node != col_node:
                deriv[row_node, col_node] = legendre[row_node] / (
                    legendre[col_node] * (nodes[row_node] - nodes[col_node])
                )
    deriv[0, 0] = -3.0
    deriv[3, 3] = 3.0
    return deriv, weights


def stencils():
    deriv, weights = gll_tables()
    stiff = np.einsum("k,kj,km->jm", weights, deriv, deriv)
    derivative = np.zeros((5, 7))
    stiffness = np.zeros((5, 7))
    for kind, holders in enumerate(((0, 3), (1,), (2,), (0,), (3,))):
        total = sum(weights[j] for j in holders)
        for j in holders:
            for m in range(4):
                derivative[kind, m - j + 3] += weights[j] * deriv[j, m] / total
                stiffness[kind, m - j + 3] += stiff[j, m] / total
    return derivative, stiffness


def by_kind(kinds, values):
    out = jnp.full(kinds.shape, float(values[0]), jnp.float32)
    for kind in range(1, len(values)):
        out = jnp.where(kinds == kind, float(values[kind]), out)
    return out


def kernel(
    sizes,
    state_hbm,
    velocity_hbm,
    wet_hbm,
    source_hbm,
    dest_hbm,
    block_hbm,
    weight_hbm,
    new,
    coupled,
    state,
    velocity,
    wet,
    source,
    dest,
    block,
    weight,
    payload,
    picked,
    pieces,
    onehot,
    fields,
    strips,
    edges,
    outbox,
    inbox,
    load_sem,
    chunk_sem,
    out_sem,
    in_sem,
    strip_sem,
    edge_sem,
):
    comps, tiles, rows, width, margins = sizes
    ocean = comps - 1
    padded = rows + 1
    parts = width // LANES
    span = parts * padded
    wide = width + LANES
    me = lax.axis_index("comp")
    tile = lax.axis_index("tile")

    def tile_at(step):
        return lax.rem(tile + step + tiles, tiles)

    def device(comp, step):
        return {"comp": comp, "tile": tile_at(step)}

    barrier = pltpu.get_barrier_semaphore()

    def greet(comp, step):
        pl.semaphore_signal(
            barrier, inc=1, device_id=device(comp, step), device_id_type=MESH
        )

    loads = [
        pltpu.make_async_copy(src, dst, load_sem.at[i])
        for i, (src, dst) in enumerate(
            (
                (source_hbm, source),
                (state_hbm.at[0, :, 0, :], state.at[0]),
                (state_hbm.at[0, :, 2, :], state.at[2]),
                (dest_hbm, dest),
                (block_hbm, block),
                (state_hbm.at[0, :, 1, :], state.at[1]),
                (state_hbm.at[0, :, 3, :], state.at[3]),
                (velocity_hbm.at[0, :, 0, :], velocity.at[0]),
                (velocity_hbm.at[0, :, 1, :], velocity.at[1]),
                (wet_hbm, wet),
            )
        )
    ]

    def chunk(i, count):
        return pltpu.make_async_copy(
            weight_hbm.at[0, 0, pl.ds(i * CHUNK, count)],
            weight.at[pl.ds(i * CHUNK, count)],
            chunk_sem.at[i],
        )

    for copy in loads:
        copy.start()
    for low in range(0, margins, CHUNK):
        chunk(low // CHUNK, min(CHUNK, margins - low)).start()

    greet(me, -1)
    greet(me, 1)

    @pl.when(me == ocean)
    def _():
        for k in range(5):
            for comp in range(ocean):
                greet(comp, k - 2)

    @pl.when(me != ocean)
    def _():
        for k in range(5):
            greet(ocean, k - 2)

    payload[...] = jnp.zeros_like(payload)
    pieces[pl.ds(margins // 8 * 8, pieces.shape[0] - margins // 8 * 8), :] = jnp.zeros(
        (pieces.shape[0] - margins // 8 * 8, 2 * LANES), jnp.float32
    )
    for copy in loads[:3]:
        copy.wait()
    for a in range(2):
        for part in range(parts):
            payload[pl.ds(part * padded, rows), pl.ds(a * LANES, LANES)] = state[
                2 * a, :, pl.ds(part * LANES, LANES)
            ]

    def place_of(numbers):
        row = (numbers * 171) >> 9
        return (numbers - 3 * row) * padded + row

    slots = lax.broadcasted_iota(jnp.int32, (span, margins), 0)
    chosen = (slots == place_of(source[0])).astype(jnp.float32)
    picked[pl.ds(0, margins), :] = lax.dot_general(
        chosen.T.astype(jnp.bfloat16),
        payload[...].astype(jnp.bfloat16),
        (((1,), (0,)), ((), ())),
        preferred_element_type=jnp.float32,
    )

    loads[3].wait()
    loads[4].wait()
    target = dest[0]
    offset = (target & (tiles - 1)) - tile + 2
    offset = jnp.where(offset < 0, offset + tiles, offset)
    offset = jnp.where(offset >= tiles, offset - tiles, offset)
    place = place_of(block[0])
    codes = offset * span + place
    codes = jnp.where(me == ocean, (target >> 5) * (5 * span) + codes, codes)
    numbers = lax.broadcasted_iota(jnp.int32, (span, margins), 0)

    def mark(slot):
        onehot[pl.ds(pl.multiple_of(slot * span, span), span), pl.ds(0, margins)] = (
            (numbers == codes - slot * span).astype(jnp.float32).astype(jnp.bfloat16)
        )

    lane = lax.broadcasted_iota(jnp.int32, (padded, LANES), 1)

    def take_fields():
        for copy in loads[5:]:
            copy.wait()
        for s in range(4):
            fields[s, pl.ds(0, rows), pl.ds(0, width)] = state[s]
        fields[4, pl.ds(0, rows), pl.ds(0, width)] = velocity[0]
        fields[5, pl.ds(0, rows), pl.ds(0, width)] = wet[...].astype(jnp.float32)
        fields[6, pl.ds(0, rows), pl.ds(0, width)] = velocity[1]
        for s in range(7):
            fields[s, pl.ds(rows, 1), pl.ds(0, width)] = jnp.zeros((1, width), jnp.float32)
        right_going = fields[0, :, pl.ds(width - LANES, LANES)]
        left_going = fields[0, :, pl.ds(0, LANES)]
        for s in range(1, 6):
            moved = pltpu.roll(fields[s, :, pl.ds(width - LANES, LANES)], LANES - 4 * s, 1)
            right_going = jnp.where(lane < LANES - 4 * s, moved, right_going)
            moved = pltpu.roll(fields[s, :, pl.ds(0, LANES)], 4 * s, 1)
            left_going = jnp.where(lane >= 4 * s, moved, left_going)
        strips[0] = right_going
        strips[1] = left_going

    rank = lax.rem(lax.broadcasted_iota(jnp.int32, (2 * GROUP, LANES), 0), GROUP)
    def multiply(low, count):
        for first in range(0, count, GROUP):
            here = min(GROUP, count - first)
            held = jnp.concatenate(
                [picked[pl.ds(low + first, GROUP), pl.ds(a * LANES, LANES)] for a in range(2)], 0
            )
            spread = jnp.concatenate(
                [jnp.where(rank == i, held, 0.0).astype(jnp.bfloat16) for i in range(here)], 1
            )
            product = jnp.dot(
                spread,
                weight[pl.ds(low + first, here)].reshape(here * LANES, LANES),
                preferred_element_type=jnp.float32,
            )
            for a in range(2):
                pieces[pl.ds(low + first, here), pl.ds(a * LANES, LANES)] = product[
                    a * GROUP : a * GROUP + here
                ]

    onehot[...] = jnp.zeros_like(onehot)
    full = margins // CHUNK
    marks = onehot.shape[0] // span // full

    def work(i, carry):
        chunk(i, CHUNK).wait()
        for j in range(marks):
            mark(i * marks + j)
        multiply(pl.multiple_of(i * CHUNK, CHUNK), CHUNK)
        return carry

    lax.fori_loop(0, full, work, 0)
    take_fields()
    chunk(full, margins - full * CHUNK).wait()
    multiply(full * CHUNK, margins - full * CHUNK)

    whole = pieces[...]
    coarse = whole.astype(jnp.bfloat16)
    fine = (whole - coarse.astype(jnp.float32)).astype(jnp.bfloat16)

    def gathered(low, count):
        held = onehot[pl.ds(low, count), :]
        return jnp.dot(held, coarse, preferred_element_type=jnp.float32) + jnp.dot(
            held, fine, preferred_element_type=jnp.float32
        )

    def message(slot, far_slot, comp, k):
        return pltpu.make_async_remote_copy(
            src_ref=outbox.at[slot],
            dst_ref=inbox.at[far_slot],
            send_sem=out_sem.at[slot],
            recv_sem=in_sem.at[far_slot],
            device_id=device(comp, k - 2),
            device_id_type=MESH,
        )

    def strip(side):
        return pltpu.make_async_remote_copy(
            src_ref=strips.at[side],
            dst_ref=edges.at[side],
            send_sem=strip_sem.at[side],
            recv_sem=edge_sem.at[side],
            device_id=device(me, 1 - 2 * side),
            device_id_type=MESH,
        )

    at_sea = me // ocean

    @pl.when(me == ocean)
    def _():
        pl.semaphore_wait(barrier, 2 + 5 * ocean)

    @pl.when(me != ocean)
    def _():
        pl.semaphore_wait(barrier, 2 + 5)

    for side in range(2):
        strip(side).start()

    def send(turn, carry):
        band = (2 * turn + 1) % ocean
        comp = at_sea * band + (1 - at_sea) * ocean
        for k in OFFSETS:
            slot = at_sea * band * 5 + k
            outbox[slot] = gathered(pl.multiple_of(slot * span, span), span)
            message(slot, (1 - at_sea) * me * 5 + k, comp, k).start()
        return carry

    lax.fori_loop(0, 1 + at_sea * (ocean - 1), send, 0)

    for side in range(2):
        strip(side).wait()

    for s in range(6):
        after = pltpu.roll(edges[1], (LANES - 4 * s) % LANES, 1)
        before = pltpu.roll(edges[0], 4 * s, 1)
        fields[s, :, pl.ds(width, LANES)] = jnp.where(
            lane == 0, after, jnp.where(lane >= LANES - 3, before, 0.0)
        )

    def total(count):
        out = None
        for slot in [comp * 5 + k for k in OFFSETS for comp in range(count // 5)]:
            pltpu.make_async_copy(inbox.at[slot], inbox.at[slot], in_sem.at[slot]).wait()
            out = inbox[slot] if out is None else out + inbox[slot]
        return out

    def give(out):
        for a in range(2):
            for part in range(parts):
                coupled[a, :, pl.ds(part * LANES, LANES)] = out[
                    part * padded : part * padded + rows, a * LANES : (a + 1) * LANES
                ]

    def sent(count):
        for slot in range(count):
            pltpu.make_async_copy(
                outbox.at[slot], outbox.at[slot], out_sem.at[slot]
            ).wait()

    @pl.when(me != ocean)
    def _():
        derivative, stiffness = stencils()
        columns = lax.rem(lax.broadcasted_iota(jnp.int32, (padded, width), 1), 3)
        row = lax.broadcasted_iota(jnp.int32, (padded, width), 0)
        row_kind = lax.rem(row, 3)
        row_kind = jnp.where(row == 0, 3, jnp.where(row == rows - 1, 4, row_kind))
        east = fields[4, :, pl.ds(0, width)]
        north = fields[6, :, pl.ds(0, width)]
        for s in range(4):
            along_x = along_y = stiff = None
            whole = fields[s]
            centre = fields[s, :, pl.ds(0, width)]
            for k in range(7):
                step = k - 3
                shifted = whole if step == 0 else pltpu.roll(whole, (-step) % wide, 1)
                shifted = shifted[:, :width]
                first = by_kind(columns, derivative[:3, k]) * shifted
                second = by_kind(columns, stiffness[:3, k]) * shifted
                shifted = centre if step == 0 else pltpu.roll(centre, (-step) % padded, 0)
                third = by_kind(row_kind, derivative[:, k]) * shifted
                second += by_kind(row_kind, stiffness[:, k]) * shifted
                along_x = first if k == 0 else along_x + first
                along_y = third if k == 0 else along_y + third
                stiff = second if k == 0 else stiff + second
            out = centre - atmos_step * (
                2.0 * (east * along_x + north * along_y) + 4.0 * viscosity * stiff
            )
            new[s] = out[:rows]
        give(total(5))
        sent(5)

    @pl.when(me == ocean)
    def _():
        p = fields[4]
        m = fields[5]
        m_centre = m[:, :width]
        q = fields[6, :, pl.ds(0, width)]
        m_x = m * pltpu.roll(m, wide - 1, 1)
        p_x = 0.25 * (p + pltpu.roll(p, wide - 1, 1))
        m_y = m_centre * pltpu.roll(m_centre, padded - 1, 0)
        q_y = 0.25 * (q + pltpu.roll(q, padded - 1, 0))
        base = []
        for s in range(4):
            u = fields[s]
            u_next = pltpu.roll(u, wide - 1, 1)
            flux = m_x * (p_x * (u + u_next) - diffusivity * (u_next - u))
            change = (flux - pltpu.roll(flux, 1, 1))[:, :width]
            u = u[:, :width]
            u_next = pltpu.roll(u, padded - 1, 0)
            flux = m_y * (q_y * (u + u_next) - diffusivity * (u_next - u))
            change = change + (flux - pltpu.roll(flux, 1, 0))
            other = fields[s ^ 1, :, pl.ds(0, width)]
            step = vertical_mix * (other - u) - change
            fields[s, :, pl.ds(0, width)] = u
            base.append(step)
        for s in (1, 3):
            u = fields[s, :, pl.ds(0, width)]
            new[s] = (u + m_centre * (ocean_step * base[s]))[:rows]
        out = total(5 * ocean)
        give(out)
        for a, coef in ((0, heat_coef), (1, salt_coef)):
            s = 2 * a
            u = fields[s, :, pl.ds(0, width)]
            surface = jnp.concatenate(
                [
                    out[part * padded : (part + 1) * padded, a * LANES : (a + 1) * LANES]
                    for part in range(parts)
                ],
                1,
            )
            step = base[s] + coef * (surface - u)
            new[s] = (u + m_centre * (ocean_step * step))[:rows]
        sent(5 * ocean)


def write(new, coupled, new_hbm, coupled_hbm, sem):
    stores = [
        pltpu.make_async_copy(slabs.at[s], out.at[0, :, s, :], sem.at[i, s])
        for i, (slabs, out) in enumerate(((new, new_hbm), (coupled, coupled_hbm)))
        for s in range(slabs.shape[0])
    ]
    for copy in stores:
        copy.start()
    for copy in stores:
        copy.wait()


def by_row(array):
    return array.transpose(0, 2, 1, 3)


def local(sizes, *arrays):
    comps, tiles, rows, width, margins = sizes
    parts = width // LANES
    padded = rows + 1
    span = parts * padded
    chunks = -(-margins // CHUNK)
    full = margins // CHUNK
    roomy = -(-margins // LANES) * LANES
    arrays = tuple(by_row(array) for array in arrays[:2]) + arrays[2:]
    state, velocity = arrays[:2]
    slots = 5 * (comps - 1)
    new, coupled = pl.pallas_call(
        functools.partial(kernel, sizes),
        out_shape=(
            pltpu.VMEM((4, rows, width), jnp.float32),
            pltpu.VMEM((2, rows, width), jnp.float32),
        ),
        in_specs=[pl.BlockSpec(memory_space=pl.ANY)] * len(arrays),
        out_specs=(pl.BlockSpec(memory_space=pltpu.VMEM),) * 2,
        scratch_shapes=[
            pltpu.VMEM((4, rows, width), jnp.float32),
            pltpu.VMEM((2, rows, width), jnp.float32),
            *[pltpu.VMEM(array.shape, array.dtype) for array in arrays[2:6]],
            pltpu.VMEM(arrays[6].shape[2:], jnp.bfloat16),
            pltpu.VMEM((span, 2 * LANES), jnp.float32),
            pltpu.VMEM((roomy, 2 * LANES), jnp.float32),
            pltpu.VMEM((roomy, 2 * LANES), jnp.float32),
            pltpu.VMEM((-(-slots // full) * full * span, roomy), jnp.bfloat16),
            pltpu.VMEM((7, padded, width + LANES), jnp.float32),
            pltpu.VMEM((2, padded, LANES), jnp.float32),
            pltpu.VMEM((2, padded, LANES), jnp.float32),
            pltpu.VMEM((slots, span, 2 * LANES), jnp.float32),
            pltpu.VMEM((slots, span, 2 * LANES), jnp.float32),
            pltpu.SemaphoreType.DMA((10,)),
            pltpu.SemaphoreType.DMA((chunks,)),
            pltpu.SemaphoreType.DMA((slots,)),
            pltpu.SemaphoreType.DMA((slots,)),
            pltpu.SemaphoreType.DMA((2,)),
            pltpu.SemaphoreType.DMA((2,)),
        ],
        compiler_params=pltpu.CompilerParams(
            collective_id=0, has_side_effects=True, vmem_limit_bytes=56 * 2**20
        ),
    )(*arrays)
    new, coupled = pl.pallas_call(
        write,
        out_shape=(
            jax.ShapeDtypeStruct(state.shape, jnp.float32),
            jax.ShapeDtypeStruct(velocity.shape, jnp.float32),
        ),
        in_specs=[pl.BlockSpec(memory_space=pltpu.VMEM)] * 2,
        out_specs=(pl.BlockSpec(memory_space=pl.ANY),) * 2,
        scratch_shapes=[pltpu.SemaphoreType.DMA((2, 4))],
        compiler_params=pltpu.CompilerParams(vmem_limit_bytes=2**20),
    )(new, coupled)
    return by_row(new), by_row(coupled)


def solution(mesh):
    comps, tiles = mesh.shape["comp"], mesh.shape["tile"]

    def whole(*arrays):
        rows, width = arrays[0].shape[2:]
        sizes = (comps, tiles, rows, width // tiles, arrays[3].shape[-1])
        placed = (
            P("comp", None, None, "tile"),
            P("comp", None, None, "tile"),
            P(None, "tile"),
            P("comp", "tile", None),
            P("comp", "tile", None),
            P("comp", "tile", None),
            P("comp", "tile", None, None, None),
        )
        return jax.shard_map(
            functools.partial(local, sizes),
            mesh=mesh,
            in_specs=placed,
            out_specs=(P("comp", None, None, "tile"), P("comp", None, None, "tile")),
            check_vma=False,
        )(*arrays)

    return whole
```

```python
import functools

import jax
import jax.numpy as jnp
import numpy as np
from jax import lax
from jax.experimental import pallas as pl
from jax.experimental.pallas import tpu as pltpu
from jax.sharding import PartitionSpec as P

MESH = pl.DeviceIdType.MESH

atmos_step = 0.02
viscosity = 0.3
ocean_step = 0.1
diffusivity = 0.2
vertical_mix = 0.5
heat_coef = 0.5
salt_coef = 0.5

LANES = 128
GROUP = 8
CHUNK = 40
OFFSETS = (0, 3, 1, 4, 2)


def gll_tables():
    nodes = np.array([-1.0, -1.0 / np.sqrt(5.0), 1.0 / np.sqrt(5.0), 1.0])
    weights = np.array([1.0 / 6.0, 5.0 / 6.0, 5.0 / 6.0, 1.0 / 6.0])
    legendre = (5.0 * nodes**3 - 3.0 * nodes) / 2.0
    deriv = np.zeros((4, 4))
    for row_node in range(4):
        for col_node in range(4):
            if row_node != col_node:
                deriv[row_node, col_node] = legendre[row_node] / (
                    legendre[col_node] * (nodes[row_node] - nodes[col_node])
                )
    deriv[0, 0] = -3.0
    deriv[3, 3] = 3.0
    return deriv, weights


def stencils():
    deriv, weights = gll_tables()
    stiff = np.einsum("k,kj,km->jm", weights, deriv, deriv)
    derivative = np.zeros((5, 7))
    stiffness = np.zeros((5, 7))
    for kind, holders in enumerate(((0, 3), (1,), (2,), (0,), (3,))):
        total = sum(weights[j] for j in holders)
        for j in holders:
            for m in range(4):
                derivative[kind, m - j + 3] += weights[j] * deriv[j, m] / total
                stiffness[kind, m - j + 3] += stiff[j, m] / total
    return derivative, stiffness


def by_kind(kinds, values):
    out = jnp.full(kinds.shape, float(values[0]), jnp.float32)
    for kind in range(1, len(values)):
        out = jnp.where(kinds == kind, float(values[kind]), out)
    return out


def kernel(
    sizes,
    state_hbm,
    velocity_hbm,
    wet_hbm,
    source_hbm,
    dest_hbm,
    block_hbm,
    weight_hbm,
    new,
    coupled,
    state,
    velocity,
    wet,
    source,
    dest,
    block,
    weight,
    payload,
    picked,
    pieces,
    onehot,
    fields,
    strips,
    edges,
    outbox,
    inbox,
    load_sem,
    chunk_sem,
    out_sem,
    in_sem,
    strip_sem,
    edge_sem,
):
    comps, tiles, rows, width, margins = sizes
    ocean = comps - 1
    padded = rows + 1
    parts = width // LANES
    span = parts * padded
    wide = width + LANES
    me = lax.axis_index("comp")
    tile = lax.axis_index("tile")

    def tile_at(step):
        return lax.rem(tile + step + tiles, tiles)

    def device(comp, step):
        return {"comp": comp, "tile": tile_at(step)}

    barrier = pltpu.get_barrier_semaphore()

    def greet(comp, step):
        pl.semaphore_signal(
            barrier, inc=1, device_id=device(comp, step), device_id_type=MESH
        )

    loads = [
        pltpu.make_async_copy(src, dst, load_sem.at[i])
        for i, (src, dst) in enumerate(
            (
                (source_hbm, source),
                (state_hbm.at[0, :, 0, :], state.at[0]),
                (state_hbm.at[0, :, 2, :], state.at[2]),
                (dest_hbm, dest),
                (block_hbm, block),
                (state_hbm.at[0, :, 1, :], state.at[1]),
                (state_hbm.at[0, :, 3, :], state.at[3]),
                (velocity_hbm.at[0, :, 0, :], velocity.at[0]),
                (velocity_hbm.at[0, :, 1, :], velocity.at[1]),
                (wet_hbm, wet),
            )
        )
    ]

    def chunk(i, count):
        return pltpu.make_async_copy(
            weight_hbm.at[0, 0, pl.ds(i * CHUNK, count)],
            weight.at[pl.ds(i * CHUNK, count)],
            chunk_sem.at[i],
        )

    for copy in loads:
        copy.start()
    for low in range(0, margins, CHUNK):
        chunk(low // CHUNK, min(CHUNK, margins - low)).start()

    greet(me, -1)
    greet(me, 1)

    @pl.when(me == ocean)
    def _():
        for k in range(5):
            for comp in range(ocean):
                greet(comp, k - 2)

    @pl.when(me != ocean)
    def _():
        for k in range(5):
            greet(ocean, k - 2)

    payload[...] = jnp.zeros_like(payload)
    pieces[pl.ds(margins // 8 * 8, pieces.shape[0] - margins // 8 * 8), :] = jnp.zeros(
        (pieces.shape[0] - margins // 8 * 8, 2 * LANES), jnp.float32
    )
    for copy in loads[:3]:
        copy.wait()
    for a in range(2):
        for part in range(parts):
            payload[pl.ds(part * padded, rows), pl.ds(a * LANES, LANES)] = state[
                2 * a, :, pl.ds(part * LANES, LANES)
            ]

    def place_of(numbers):
        row = (numbers * 171) >> 9
        return (numbers - 3 * row) * padded + row

    slots = lax.broadcasted_iota(jnp.int32, (span, margins), 0)
    chosen = (slots == place_of(source[0])).astype(jnp.float32)
    picked[pl.ds(0, margins), :] = lax.dot_general(
        chosen.T.astype(jnp.bfloat16),
        payload[...].astype(jnp.bfloat16),
        (((1,), (0,)), ((), ())),
        preferred_element_type=jnp.float32,
    )

    loads[3].wait()
    loads[4].wait()
    target = dest[0]
    offset = (target & (tiles - 1)) - tile + 2
    offset = jnp.where(offset < 0, offset + tiles, offset)
    offset = jnp.where(offset >= tiles, offset - tiles, offset)
    place = place_of(block[0])
    codes = offset * span + place
    codes = jnp.where(me == ocean, (target >> 5) * (5 * span) + codes, codes)
    numbers = lax.broadcasted_iota(jnp.int32, (span, margins), 0)

    def mark(slot):
        onehot[pl.ds(pl.multiple_of(slot * span, span), span), pl.ds(0, margins)] = (
            (numbers == codes - slot * span).astype(jnp.float32).astype(jnp.bfloat16)
        )

    lane = lax.broadcasted_iota(jnp.int32, (padded, LANES), 1)

    def take_fields():
        for copy in loads[5:]:
            copy.wait()
        for s in range(4):
            fields[s, pl.ds(0, rows), pl.ds(0, width)] = state[s]
        fields[4, pl.ds(0, rows), pl.ds(0, width)] = velocity[0]
        fields[5, pl.ds(0, rows), pl.ds(0, width)] = wet[...].astype(jnp.float32)
        fields[6, pl.ds(0, rows), pl.ds(0, width)] = velocity[1]
        for s in range(7):
            fields[s, pl.ds(rows, 1), pl.ds(0, width)] = jnp.zeros((1, width), jnp.float32)
        right_going = fields[0, :, pl.ds(width - LANES, LANES)]
        left_going = fields[0, :, pl.ds(0, LANES)]
        for s in range(1, 6):
            moved = pltpu.roll(fields[s, :, pl.ds(width - LANES, LANES)], LANES - 4 * s, 1)
            right_going = jnp.where(lane < LANES - 4 * s, moved, right_going)
            moved = pltpu.roll(fields[s, :, pl.ds(0, LANES)], 4 * s, 1)
            left_going = jnp.where(lane >= 4 * s, moved, left_going)
        strips[0] = right_going
        strips[1] = left_going

    rank = lax.rem(lax.broadcasted_iota(jnp.int32, (2 * GROUP, LANES), 0), GROUP)
    def multiply(low, count):
        for first in range(0, count, GROUP):
            here = min(GROUP, count - first)
            held = jnp.concatenate(
                [picked[pl.ds(low + first, GROUP), pl.ds(a * LANES, LANES)] for a in range(2)], 0
            )
            spread = jnp.concatenate(
                [jnp.where(rank == i, held, 0.0).astype(jnp.bfloat16) for i in range(here)], 1
            )
            product = jnp.dot(
                spread,
                weight[pl.ds(low + first, here)].reshape(here * LANES, LANES),
                preferred_element_type=jnp.float32,
            )
            for a in range(2):
                pieces[pl.ds(low + first, here), pl.ds(a * LANES, LANES)] = product[
                    a * GROUP : a * GROUP + here
                ]

    onehot[...] = jnp.zeros_like(onehot)
    full = margins // CHUNK
    marks = onehot.shape[0] // span // full

    def work(i, carry):
        chunk(i, CHUNK).wait()
        for j in range(marks):
            mark(i * marks + j)
        multiply(pl.multiple_of(i * CHUNK, CHUNK), CHUNK)
        return carry

    lax.fori_loop(0, full, work, 0)
    take_fields()
    chunk(full, margins - full * CHUNK).wait()
    multiply(full * CHUNK, margins - full * CHUNK)

    whole = pieces[...]
    coarse = whole.astype(jnp.bfloat16)
    fine = (whole - coarse.astype(jnp.float32)).astype(jnp.bfloat16)

    def gathered(low, count):
        held = onehot[pl.ds(low, count), :]
        return jnp.dot(held, coarse, preferred_element_type=jnp.float32) + jnp.dot(
            held, fine, preferred_element_type=jnp.float32
        )

    def message(slot, far_slot, comp, k):
        return pltpu.make_async_remote_copy(
            src_ref=outbox.at[slot],
            dst_ref=inbox.at[far_slot],
            send_sem=out_sem.at[slot],
            recv_sem=in_sem.at[far_slot],
            device_id=device(comp, k - 2),
            device_id_type=MESH,
        )

    def strip(side):
        return pltpu.make_async_remote_copy(
            src_ref=strips.at[side],
            dst_ref=edges.at[side],
            send_sem=strip_sem.at[side],
            recv_sem=edge_sem.at[side],
            device_id=device(me, 1 - 2 * side),
            device_id_type=MESH,
        )

    at_sea = me // ocean

    @pl.when(me == ocean)
    def _():
        pl.semaphore_wait(barrier, 2 + 5 * ocean)

    @pl.when(me != ocean)
    def _():
        pl.semaphore_wait(barrier, 2 + 5)

    for side in range(2):
        strip(side).start()

    def send(turn, carry):
        band = (2 * turn + 1) % ocean
        comp = at_sea * band + (1 - at_sea) * ocean
        start = at_sea * band * 5
        every = gathered(pl.multiple_of(start * span, span), 5 * span)
        for k in OFFSETS:
            slot = start + k
            outbox[slot] = every[k * span : (k + 1) * span]
            message(slot, (1 - at_sea) * me * 5 + k, comp, k).start()
        return carry

    lax.fori_loop(0, 1 + at_sea * (ocean - 1), send, 0)

    for side in range(2):
        strip(side).wait()

    for s in range(6):
        after = pltpu.roll(edges[1], (LANES - 4 * s) % LANES, 1)
        before = pltpu.roll(edges[0], 4 * s, 1)
        fields[s, :, pl.ds(width, LANES)] = jnp.where(
            lane == 0, after, jnp.where(lane >= LANES - 3, before, 0.0)
        )

    def total(count):
        out = None
        for slot in [comp * 5 + k for k in OFFSETS for comp in range(count // 5)]:
            pltpu.make_async_copy(inbox.at[slot], inbox.at[slot], in_sem.at[slot]).wait()
            out = inbox[slot] if out is None else out + inbox[slot]
        return out

    def give(out):
        for a in range(2):
            for part in range(parts):
                coupled[a, :, pl.ds(part * LANES, LANES)] = out[
                    part * padded : part * padded + rows, a * LANES : (a + 1) * LANES
                ]

    def sent(count):
        for slot in range(count):
            pltpu.make_async_copy(
                outbox.at[slot], outbox.at[slot], out_sem.at[slot]
            ).wait()

    @pl.when(me != ocean)
    def _():
        derivative, stiffness = stencils()
        columns = lax.rem(lax.broadcasted_iota(jnp.int32, (padded, width), 1), 3)
        row = lax.broadcasted_iota(jnp.int32, (padded, width), 0)
        row_kind = lax.rem(row, 3)
        row_kind = jnp.where(row == 0, 3, jnp.where(row == rows - 1, 4, row_kind))
        east = fields[4, :, pl.ds(0, width)]
        north = fields[6, :, pl.ds(0, width)]
        for s in range(4):
            along_x = along_y = stiff = None
            whole = fields[s]
            centre = fields[s, :, pl.ds(0, width)]
            for k in range(7):
                step = k - 3
                shifted = whole if step == 0 else pltpu.roll(whole, (-step) % wide, 1)
                shifted = shifted[:, :width]
                first = by_kind(columns, derivative[:3, k]) * shifted
                second = by_kind(columns, stiffness[:3, k]) * shifted
                shifted = centre if step == 0 else pltpu.roll(centre, (-step) % padded, 0)
                third = by_kind(row_kind, derivative[:, k]) * shifted
                second += by_kind(row_kind, stiffness[:, k]) * shifted
                along_x = first if k == 0 else along_x + first
                along_y = third if k == 0 else along_y + third
                stiff = second if k == 0 else stiff + second
            out = centre - atmos_step * (
                2.0 * (east * along_x + north * along_y) + 4.0 * viscosity * stiff
            )
            new[s] = out[:rows]
        give(total(5))
        sent(5)

    @pl.when(me == ocean)
    def _():
        p = fields[4]
        m = fields[5]
        m_centre = m[:, :width]
        q = fields[6, :, pl.ds(0, width)]
        m_x = m * pltpu.roll(m, wide - 1, 1)
        p_x = 0.25 * (p + pltpu.roll(p, wide - 1, 1))
        m_y = m_centre * pltpu.roll(m_centre, padded - 1, 0)
        q_y = 0.25 * (q + pltpu.roll(q, padded - 1, 0))
        base = []
        for s in range(4):
            u = fields[s]
            u_next = pltpu.roll(u, wide - 1, 1)
            flux = m_x * (p_x * (u + u_next) - diffusivity * (u_next - u))
            change = (flux - pltpu.roll(flux, 1, 1))[:, :width]
            u = u[:, :width]
            u_next = pltpu.roll(u, padded - 1, 0)
            flux = m_y * (q_y * (u + u_next) - diffusivity * (u_next - u))
            change = change + (flux - pltpu.roll(flux, 1, 0))
            other = fields[s ^ 1, :, pl.ds(0, width)]
            step = vertical_mix * (other - u) - change
            fields[s, :, pl.ds(0, width)] = u
            base.append(step)
        for s in (1, 3):
            u = fields[s, :, pl.ds(0, width)]
            new[s] = (u + m_centre * (ocean_step * base[s]))[:rows]
        out = total(5 * ocean)
        give(out)
        for a, coef in ((0, heat_coef), (1, salt_coef)):
            s = 2 * a
            u = fields[s, :, pl.ds(0, width)]
            surface = jnp.concatenate(
                [
                    out[part * padded : (part + 1) * padded, a * LANES : (a + 1) * LANES]
                    for part in range(parts)
                ],
                1,
            )
            step = base[s] + coef * (surface - u)
            new[s] = (u + m_centre * (ocean_step * step))[:rows]
        sent(5 * ocean)


def write(new, coupled, new_hbm, coupled_hbm, sem):
    stores = [
        pltpu.make_async_copy(slabs.at[s], out.at[0, :, s, :], sem.at[i, s])
        for i, (slabs, out) in enumerate(((new, new_hbm), (coupled, coupled_hbm)))
        for s in range(slabs.shape[0])
    ]
    for copy in stores:
        copy.start()
    for copy in stores:
        copy.wait()


def by_row(array):
    return array.transpose(0, 2, 1, 3)


def local(sizes, *arrays):
    comps, tiles, rows, width, margins = sizes
    parts = width // LANES
    padded = rows + 1
    span = parts * padded
    chunks = -(-margins // CHUNK)
    full = margins // CHUNK
    roomy = -(-margins // LANES) * LANES
    arrays = tuple(by_row(array) for array in arrays[:2]) + arrays[2:]
    state, velocity = arrays[:2]
    slots = 5 * (comps - 1)
    new, coupled = pl.pallas_call(
        functools.partial(kernel, sizes),
        out_shape=(
            pltpu.VMEM((4, rows, width), jnp.float32),
            pltpu.VMEM((2, rows, width), jnp.float32),
        ),
        in_specs=[pl.BlockSpec(memory_space=pl.ANY)] * len(arrays),
        out_specs=(pl.BlockSpec(memory_space=pltpu.VMEM),) * 2,
        scratch_shapes=[
            pltpu.VMEM((4, rows, width), jnp.float32),
            pltpu.VMEM((2, rows, width), jnp.float32),
            *[pltpu.VMEM(array.shape, array.dtype) for array in arrays[2:6]],
            pltpu.VMEM(arrays[6].shape[2:], jnp.bfloat16),
            pltpu.VMEM((span, 2 * LANES), jnp.float32),
            pltpu.VMEM((roomy, 2 * LANES), jnp.float32),
            pltpu.VMEM((roomy, 2 * LANES), jnp.float32),
            pltpu.VMEM((-(-slots // full) * full * span, roomy), jnp.bfloat16),
            pltpu.VMEM((7, padded, width + LANES), jnp.float32),
            pltpu.VMEM((2, padded, LANES), jnp.float32),
            pltpu.VMEM((2, padded, LANES), jnp.float32),
            pltpu.VMEM((slots, span, 2 * LANES), jnp.float32),
            pltpu.VMEM((slots, span, 2 * LANES), jnp.float32),
            pltpu.SemaphoreType.DMA((10,)),
            pltpu.SemaphoreType.DMA((chunks,)),
            pltpu.SemaphoreType.DMA((slots,)),
            pltpu.SemaphoreType.DMA((slots,)),
            pltpu.SemaphoreType.DMA((2,)),
            pltpu.SemaphoreType.DMA((2,)),
        ],
        compiler_params=pltpu.CompilerParams(
            collective_id=0, has_side_effects=True, vmem_limit_bytes=56 * 2**20
        ),
    )(*arrays)
    new, coupled = pl.pallas_call(
        write,
        out_shape=(
            jax.ShapeDtypeStruct(state.shape, jnp.float32),
            jax.ShapeDtypeStruct(velocity.shape, jnp.float32),
        ),
        in_specs=[pl.BlockSpec(memory_space=pltpu.VMEM)] * 2,
        out_specs=(pl.BlockSpec(memory_space=pl.ANY),) * 2,
        scratch_shapes=[pltpu.SemaphoreType.DMA((2, 4))],
        compiler_params=pltpu.CompilerParams(vmem_limit_bytes=2**20),
    )(new, coupled)
    return by_row(new), by_row(coupled)


def solution(mesh):
    comps, tiles = mesh.shape["comp"], mesh.shape["tile"]

    def whole(*arrays):
        rows, width = arrays[0].shape[2:]
        sizes = (comps, tiles, rows, width // tiles, arrays[3].shape[-1])
        placed = (
            P("comp", None, None, "tile"),
            P("comp", None, None, "tile"),
            P(None, "tile"),
            P("comp", "tile", None),
            P("comp", "tile", None),
            P("comp", "tile", None),
            P("comp", "tile", None, None, None),
        )
        return jax.shard_map(
            functools.partial(local, sizes),
            mesh=mesh,
            in_specs=placed,
            out_specs=(P("comp", None, None, "tile"), P("comp", None, None, "tile")),
            check_vma=False,
        )(*arrays)

    return whole
```

```python
import functools

import jax
import jax.numpy as jnp
import numpy as np
from jax import lax
from jax.experimental import pallas as pl
from jax.experimental.pallas import tpu as pltpu
from jax.sharding import PartitionSpec as P

MESH = pl.DeviceIdType.MESH

atmos_step = 0.02
viscosity = 0.3
ocean_step = 0.1
diffusivity = 0.2
vertical_mix = 0.5
heat_coef = 0.5
salt_coef = 0.5

LANES = 128
GROUP = 8
CHUNK = 40
OFFSETS = (0, 3, 1, 4, 2)


def gll_tables():
    nodes = np.array([-1.0, -1.0 / np.sqrt(5.0), 1.0 / np.sqrt(5.0), 1.0])
    weights = np.array([1.0 / 6.0, 5.0 / 6.0, 5.0 / 6.0, 1.0 / 6.0])
    legendre = (5.0 * nodes**3 - 3.0 * nodes) / 2.0
    deriv = np.zeros((4, 4))
    for row_node in range(4):
        for col_node in range(4):
            if row_node != col_node:
                deriv[row_node, col_node] = legendre[row_node] / (
                    legendre[col_node] * (nodes[row_node] - nodes[col_node])
                )
    deriv[0, 0] = -3.0
    deriv[3, 3] = 3.0
    return deriv, weights


def stencils():
    deriv, weights = gll_tables()
    stiff = np.einsum("k,kj,km->jm", weights, deriv, deriv)
    derivative = np.zeros((5, 7))
    stiffness = np.zeros((5, 7))
    for kind, holders in enumerate(((0, 3), (1,), (2,), (0,), (3,))):
        total = sum(weights[j] for j in holders)
        for j in holders:
            for m in range(4):
                derivative[kind, m - j + 3] += weights[j] * deriv[j, m] / total
                stiffness[kind, m - j + 3] += stiff[j, m] / total
    return derivative, stiffness


def by_kind(kinds, values):
    out = jnp.full(kinds.shape, float(values[0]), jnp.float32)
    for kind in range(1, len(values)):
        out = jnp.where(kinds == kind, float(values[kind]), out)
    return out


def kernel(
    sizes,
    state_hbm,
    velocity_hbm,
    wet_hbm,
    source_hbm,
    dest_hbm,
    block_hbm,
    weight_hbm,
    new,
    coupled,
    state,
    velocity,
    wet,
    source,
    dest,
    block,
    weight,
    payload,
    picked,
    pieces,
    onehot,
    fields,
    strips,
    edges,
    outbox,
    inbox,
    load_sem,
    chunk_sem,
    out_sem,
    in_sem,
    strip_sem,
    edge_sem,
):
    comps, tiles, rows, width, margins = sizes
    ocean = comps - 1
    padded = rows + 1
    parts = width // LANES
    span = parts * padded
    wide = width + LANES
    me = lax.axis_index("comp")
    tile = lax.axis_index("tile")

    def tile_at(step):
        return lax.rem(tile + step + tiles, tiles)

    def device(comp, step):
        return {"comp": comp, "tile": tile_at(step)}

    barrier = pltpu.get_barrier_semaphore()

    def greet(comp, step):
        pl.semaphore_signal(
            barrier, inc=1, device_id=device(comp, step), device_id_type=MESH
        )

    loads = [
        pltpu.make_async_copy(src, dst, load_sem.at[i])
        for i, (src, dst) in enumerate(
            (
                (dest_hbm, dest),
                (block_hbm, block),
                (source_hbm, source),
                (state_hbm.at[0, :, 0, :], state.at[0]),
                (state_hbm.at[0, :, 2, :], state.at[2]),
                (state_hbm.at[0, :, 1, :], state.at[1]),
                (state_hbm.at[0, :, 3, :], state.at[3]),
                (velocity_hbm.at[0, :, 0, :], velocity.at[0]),
                (velocity_hbm.at[0, :, 1, :], velocity.at[1]),
                (wet_hbm, wet),
            )
        )
    ]

    def chunk(i, count):
        return pltpu.make_async_copy(
            weight_hbm.at[0, 0, pl.ds(i * CHUNK, count)],
            weight.at[pl.ds(i * CHUNK, count)],
            chunk_sem.at[i],
        )

    for copy in loads:
        copy.start()
    for low in range(0, margins, CHUNK):
        chunk(low // CHUNK, min(CHUNK, margins - low)).start()

    greet(me, -1)
    greet(me, 1)

    @pl.when(me == ocean)
    def _():
        for k in range(5):
            for comp in range(ocean):
                greet(comp, k - 2)

    @pl.when(me != ocean)
    def _():
        for k in range(5):
            greet(ocean, k - 2)

    payload[...] = jnp.zeros_like(payload)
    pieces[pl.ds(margins // 8 * 8, pieces.shape[0] - margins // 8 * 8), :] = jnp.zeros(
        (pieces.shape[0] - margins // 8 * 8, 2 * LANES), jnp.float32
    )
    def place_of(numbers):
        row = (numbers * 171) >> 9
        return (numbers - 3 * row) * padded + row

    loads[0].wait()
    loads[1].wait()
    target = dest[0]
    offset = (target & (tiles - 1)) - tile + 2
    offset = jnp.where(offset < 0, offset + tiles, offset)
    offset = jnp.where(offset >= tiles, offset - tiles, offset)
    place = place_of(block[0])
    codes = offset * span + place
    codes = jnp.where(me == ocean, (target >> 5) * (5 * span) + codes, codes)
    numbers = lax.broadcasted_iota(jnp.int32, (span, margins), 0)

    def mark(slot):
        onehot[pl.ds(pl.multiple_of(slot * span, span), span), pl.ds(0, margins)] = (
            (numbers == codes - slot * span).astype(jnp.float32).astype(jnp.bfloat16)
        )

    last = margins // LANES * LANES
    onehot[:, pl.ds(last, onehot.shape[1] - last)] = jnp.zeros(
        (onehot.shape[0], onehot.shape[1] - last), jnp.bfloat16
    )

    def mark_band(band, carry):
        for k in range(5):
            mark(band * 5 + k)
        return carry

    lax.fori_loop(0, 1 + me // ocean * (ocean - 1), mark_band, 0)

    loads[2].wait()
    slots = lax.broadcasted_iota(jnp.int32, (span, margins), 0)
    chosen = (slots == place_of(source[0])).astype(jnp.float32)
    chosen = chosen.T.astype(jnp.bfloat16)

    for copy in loads[3:5]:
        copy.wait()
    for a in range(2):
        for part in range(parts):
            payload[pl.ds(part * padded, rows), pl.ds(a * LANES, LANES)] = state[
                2 * a, :, pl.ds(part * LANES, LANES)
            ]

    picked[pl.ds(0, margins), :] = lax.dot_general(
        chosen,
        payload[...].astype(jnp.bfloat16),
        (((1,), (0,)), ((), ())),
        preferred_element_type=jnp.float32,
    )

    lane = lax.broadcasted_iota(jnp.int32, (padded, LANES), 1)

    def take_fields():
        for copy in loads[5:]:
            copy.wait()
        for s in range(4):
            fields[s, pl.ds(0, rows), pl.ds(0, width)] = state[s]
        fields[4, pl.ds(0, rows), pl.ds(0, width)] = velocity[0]
        fields[5, pl.ds(0, rows), pl.ds(0, width)] = wet[...].astype(jnp.float32)
        fields[6, pl.ds(0, rows), pl.ds(0, width)] = velocity[1]
        for s in range(7):
            fields[s, pl.ds(rows, 1), pl.ds(0, width)] = jnp.zeros((1, width), jnp.float32)
        right_going = fields[0, :, pl.ds(width - LANES, LANES)]
        left_going = fields[0, :, pl.ds(0, LANES)]
        for s in range(1, 6):
            moved = pltpu.roll(fields[s, :, pl.ds(width - LANES, LANES)], LANES - 4 * s, 1)
            right_going = jnp.where(lane < LANES - 4 * s, moved, right_going)
            moved = pltpu.roll(fields[s, :, pl.ds(0, LANES)], 4 * s, 1)
            left_going = jnp.where(lane >= 4 * s, moved, left_going)
        strips[0] = right_going
        strips[1] = left_going

    rank = lax.rem(lax.broadcasted_iota(jnp.int32, (2 * GROUP, LANES), 0), GROUP)
    def multiply(low, count):
        for first in range(0, count, GROUP):
            here = min(GROUP, count - first)
            held = jnp.concatenate(
                [picked[pl.ds(low + first, GROUP), pl.ds(a * LANES, LANES)] for a in range(2)], 0
            )
            spread = jnp.concatenate(
                [jnp.where(rank == i, held, 0.0).astype(jnp.bfloat16) for i in range(here)], 1
            )
            product = jnp.dot(
                spread,
                weight[pl.ds(low + first, here)].reshape(here * LANES, LANES),
                preferred_element_type=jnp.float32,
            )
            for a in range(2):
                pieces[pl.ds(low + first, here), pl.ds(a * LANES, LANES)] = product[
                    a * GROUP : a * GROUP + here
                ]

    full = margins // CHUNK

    def work(i, carry):
        chunk(i, CHUNK).wait()
        multiply(pl.multiple_of(i * CHUNK, CHUNK), CHUNK)
        return carry

    lax.fori_loop(0, full, work, 0)
    take_fields()
    chunk(full, margins - full * CHUNK).wait()
    multiply(full * CHUNK, margins - full * CHUNK)

    whole = pieces[...]
    coarse = whole.astype(jnp.bfloat16)
    fine = (whole - coarse.astype(jnp.float32)).astype(jnp.bfloat16)

    def gathered(low, count):
        held = onehot[pl.ds(low, count), :]
        return jnp.dot(held, coarse, preferred_element_type=jnp.float32) + jnp.dot(
            held, fine, preferred_element_type=jnp.float32
        )

    def message(slot, far_slot, comp, k):
        return pltpu.make_async_remote_copy(
            src_ref=outbox.at[slot],
            dst_ref=inbox.at[far_slot],
            send_sem=out_sem.at[slot],
            recv_sem=in_sem.at[far_slot],
            device_id=device(comp, k - 2),
            device_id_type=MESH,
        )

    def strip(side):
        return pltpu.make_async_remote_copy(
            src_ref=strips.at[side],
            dst_ref=edges.at[side],
            send_sem=strip_sem.at[side],
            recv_sem=edge_sem.at[side],
            device_id=device(me, 1 - 2 * side),
            device_id_type=MESH,
        )

    at_sea = me // ocean

    @pl.when(me == ocean)
    def _():
        pl.semaphore_wait(barrier, 2 + 5 * ocean)

    @pl.when(me != ocean)
    def _():
        pl.semaphore_wait(barrier, 2 + 5)

    for side in range(2):
        strip(side).start()

    def send(turn, carry):
        band = (2 * turn + 1) % ocean
        comp = at_sea * band + (1 - at_sea) * ocean
        start = at_sea * band * 5
        every = gathered(pl.multiple_of(start * span, span), 5 * span)
        for k in OFFSETS:
            slot = start + k
            outbox[slot] = every[k * span : (k + 1) * span]
            message(slot, (1 - at_sea) * me * 5 + k, comp, k).start()
        return carry

    lax.fori_loop(0, 1 + at_sea * (ocean - 1), send, 0)

    for side in range(2):
        strip(side).wait()

    for s in range(6):
        after = pltpu.roll(edges[1], (LANES - 4 * s) % LANES, 1)
        before = pltpu.roll(edges[0], 4 * s, 1)
        fields[s, :, pl.ds(width, LANES)] = jnp.where(
            lane == 0, after, jnp.where(lane >= LANES - 3, before, 0.0)
        )

    def total(count):
        out = None
        for slot in [comp * 5 + k for k in OFFSETS for comp in range(count // 5)]:
            pltpu.make_async_copy(inbox.at[slot], inbox.at[slot], in_sem.at[slot]).wait()
            out = inbox[slot] if out is None else out + inbox[slot]
        return out

    def give(out):
        for a in range(2):
            for part in range(parts):
                coupled[a, :, pl.ds(part * LANES, LANES)] = out[
                    part * padded : part * padded + rows, a * LANES : (a + 1) * LANES
                ]

    def sent(count):
        for slot in range(count):
            pltpu.make_async_copy(
                outbox.at[slot], outbox.at[slot], out_sem.at[slot]
            ).wait()

    @pl.when(me != ocean)
    def _():
        derivative, stiffness = stencils()
        columns = lax.rem(lax.broadcasted_iota(jnp.int32, (padded, width), 1), 3)
        row = lax.broadcasted_iota(jnp.int32, (padded, width), 0)
        row_kind = lax.rem(row, 3)
        row_kind = jnp.where(row == 0, 3, jnp.where(row == rows - 1, 4, row_kind))
        east = fields[4, :, pl.ds(0, width)]
        north = fields[6, :, pl.ds(0, width)]
        for s in range(4):
            along_x = along_y = stiff = None
            whole = fields[s]
            centre = fields[s, :, pl.ds(0, width)]
            for k in range(7):
                step = k - 3
                shifted = whole if step == 0 else pltpu.roll(whole, (-step) % wide, 1)
                shifted = shifted[:, :width]
                first = by_kind(columns, derivative[:3, k]) * shifted
                second = by_kind(columns, stiffness[:3, k]) * shifted
                shifted = centre if step == 0 else pltpu.roll(centre, (-step) % padded, 0)
                third = by_kind(row_kind, derivative[:, k]) * shifted
                second += by_kind(row_kind, stiffness[:, k]) * shifted
                along_x = first if k == 0 else along_x + first
                along_y = third if k == 0 else along_y + third
                stiff = second if k == 0 else stiff + second
            out = centre - atmos_step * (
                2.0 * (east * along_x + north * along_y) + 4.0 * viscosity * stiff
            )
            new[s] = out[:rows]
        give(total(5))
        sent(5)

    @pl.when(me == ocean)
    def _():
        p = fields[4]
        m = fields[5]
        m_centre = m[:, :width]
        q = fields[6, :, pl.ds(0, width)]
        m_x = m * pltpu.roll(m, wide - 1, 1)
        p_x = 0.25 * (p + pltpu.roll(p, wide - 1, 1))
        m_y = m_centre * pltpu.roll(m_centre, padded - 1, 0)
        q_y = 0.25 * (q + pltpu.roll(q, padded - 1, 0))
        base = []
        for s in range(4):
            u = fields[s]
            u_next = pltpu.roll(u, wide - 1, 1)
            flux = m_x * (p_x * (u + u_next) - diffusivity * (u_next - u))
            change = (flux - pltpu.roll(flux, 1, 1))[:, :width]
            u = u[:, :width]
            u_next = pltpu.roll(u, padded - 1, 0)
            flux = m_y * (q_y * (u + u_next) - diffusivity * (u_next - u))
            change = change + (flux - pltpu.roll(flux, 1, 0))
            other = fields[s ^ 1, :, pl.ds(0, width)]
            step = vertical_mix * (other - u) - change
            fields[s, :, pl.ds(0, width)] = u
            base.append(step)
        for s in (1, 3):
            u = fields[s, :, pl.ds(0, width)]
            new[s] = (u + m_centre * (ocean_step * base[s]))[:rows]
        out = total(5 * ocean)
        give(out)
        for a, coef in ((0, heat_coef), (1, salt_coef)):
            s = 2 * a
            u = fields[s, :, pl.ds(0, width)]
            surface = jnp.concatenate(
                [
                    out[part * padded : (part + 1) * padded, a * LANES : (a + 1) * LANES]
                    for part in range(parts)
                ],
                1,
            )
            step = base[s] + coef * (surface - u)
            new[s] = (u + m_centre * (ocean_step * step))[:rows]
        sent(5 * ocean)


def write(new, coupled, new_hbm, coupled_hbm, sem):
    stores = [
        pltpu.make_async_copy(slabs.at[s], out.at[0, :, s, :], sem.at[i, s])
        for i, (slabs, out) in enumerate(((new, new_hbm), (coupled, coupled_hbm)))
        for s in range(slabs.shape[0])
    ]
    for copy in stores:
        copy.start()
    for copy in stores:
        copy.wait()


def by_row(array):
    return array.transpose(0, 2, 1, 3)


def local(sizes, *arrays):
    comps, tiles, rows, width, margins = sizes
    parts = width // LANES
    padded = rows + 1
    span = parts * padded
    chunks = -(-margins // CHUNK)
    roomy = -(-margins // LANES) * LANES
    arrays = tuple(by_row(array) for array in arrays[:2]) + arrays[2:]
    state, velocity = arrays[:2]
    slots = 5 * (comps - 1)
    new, coupled = pl.pallas_call(
        functools.partial(kernel, sizes),
        out_shape=(
            pltpu.VMEM((4, rows, width), jnp.float32),
            pltpu.VMEM((2, rows, width), jnp.float32),
        ),
        in_specs=[pl.BlockSpec(memory_space=pl.ANY)] * len(arrays),
        out_specs=(pl.BlockSpec(memory_space=pltpu.VMEM),) * 2,
        scratch_shapes=[
            pltpu.VMEM((4, rows, width), jnp.float32),
            pltpu.VMEM((2, rows, width), jnp.float32),
            *[pltpu.VMEM(array.shape, array.dtype) for array in arrays[2:6]],
            pltpu.VMEM(arrays[6].shape[2:], jnp.bfloat16),
            pltpu.VMEM((span, 2 * LANES), jnp.float32),
            pltpu.VMEM((roomy, 2 * LANES), jnp.float32),
            pltpu.VMEM((roomy, 2 * LANES), jnp.float32),
            pltpu.VMEM((slots * span, roomy), jnp.bfloat16),
            pltpu.VMEM((7, padded, width + LANES), jnp.float32),
            pltpu.VMEM((2, padded, LANES), jnp.float32),
            pltpu.VMEM((2, padded, LANES), jnp.float32),
            pltpu.VMEM((slots, span, 2 * LANES), jnp.float32),
            pltpu.VMEM((slots, span, 2 * LANES), jnp.float32),
            pltpu.SemaphoreType.DMA((10,)),
            pltpu.SemaphoreType.DMA((chunks,)),
            pltpu.SemaphoreType.DMA((slots,)),
            pltpu.SemaphoreType.DMA((slots,)),
            pltpu.SemaphoreType.DMA((2,)),
            pltpu.SemaphoreType.DMA((2,)),
        ],
        compiler_params=pltpu.CompilerParams(
            collective_id=0, has_side_effects=True, vmem_limit_bytes=56 * 2**20
        ),
    )(*arrays)
    new, coupled = pl.pallas_call(
        write,
        out_shape=(
            jax.ShapeDtypeStruct(state.shape, jnp.float32),
            jax.ShapeDtypeStruct(velocity.shape, jnp.float32),
        ),
        in_specs=[pl.BlockSpec(memory_space=pltpu.VMEM)] * 2,
        out_specs=(pl.BlockSpec(memory_space=pl.ANY),) * 2,
        scratch_shapes=[pltpu.SemaphoreType.DMA((2, 4))],
        compiler_params=pltpu.CompilerParams(vmem_limit_bytes=2**20),
    )(new, coupled)
    return by_row(new), by_row(coupled)


def solution(mesh):
    comps, tiles = mesh.shape["comp"], mesh.shape["tile"]

    def whole(*arrays):
        rows, width = arrays[0].shape[2:]
        sizes = (comps, tiles, rows, width // tiles, arrays[3].shape[-1])
        placed = (
            P("comp", None, None, "tile"),
            P("comp", None, None, "tile"),
            P(None, "tile"),
            P("comp", "tile", None),
            P("comp", "tile", None),
            P("comp", "tile", None),
            P("comp", "tile", None, None, None),
        )
        return jax.shard_map(
            functools.partial(local, sizes),
            mesh=mesh,
            in_specs=placed,
            out_specs=(P("comp", None, None, "tile"), P("comp", None, None, "tile")),
            check_vma=False,
        )(*arrays)

    return whole
```
